128 devices in a mesh: pipe: 8 (over x, y_hi), expert: 2 (over core), dp: 8 (over y_lo, z).
Axes of the slice: x: 4, y: 4 (y_hi: 2, y_lo: 2; y = y_hi * 2 + y_lo), z: 4, core: 2. Of those that a mesh axis runs over, the one named last changes fastest.
Arguments:
- hidden_in: bfloat16 [16384, 6144], P(('pipe', 'expert', 'dp'))
- norm_gain: float32 [8, 6144], P('pipe'), may hold values from 0.1 to 1.9
- w_gate: bfloat16 [8, 6144, 8192], P('pipe', None, ('expert', 'dp')), may hold values from -0.078125 to 0.078125
- w_up: bfloat16 [8, 6144, 8192], P('pipe', None, ('expert', 'dp')), may hold values from -0.078125 to 0.078125
- w_down: bfloat16 [8, 8192, 6144], P('pipe', ('expert', 'dp')), may hold values from -0.0625 to 0.0625
- expert_ids: int32 [16384, 2], P(('pipe', 'expert', 'dp')), may hold values from 0 to 7, as said below
- gate_weights: float32 [16384, 2], P(('pipe', 'expert', 'dp')), may hold values from 0.25 to 1
Outputs:
- passed_on: bfloat16 [16384, 6144], P(('pipe', 'expert', 'dp'))
The draws below stay inside these ranges and needn't reach their ends.
Inputs may be any that keep to these rules, and one draw needn't show every extreme that they name: `expert_ids`: the two ids of a row differ. In every aligned block of 128 rows (the rows of one device) at most 64 rows name expert 0, and in each section's 16 blocks at least one block has 64 such rows; the 16 blocks of one section hold exactly 512 rows that name expert 0.
All inputs are finite; a program needn't handle non-finite values.
Results may differ from the reference program's by a relative error of at most 0.0045.
Values may be sent and summed in bfloat16 or wider, within the bound.
A program may use at most 192 MiB of HBM per device.

```python
import math
import jax
import jax.numpy as jnp
from jax import lax

D = 6144
FF_WIN = 8192
EXPERTS = 8
TOP = 2
TOK_DEV = 128
CAP = 64
GROUP = 16
SECTIONS = 8
TOKENS = 16384


def draw_hidden_in(key, part):
    key = jax.random.fold_in(key, 5)
    key_base, key_row, key_col = jax.random.split(key, 3)
    base = jax.random.normal(key_base, (TOKENS, D), jnp.float32)
    row_scale = jnp.exp(jax.random.uniform(key_row, (TOKENS, 1), jnp.float32, math.log(0.3), math.log(3.0)))
    col_scale = jnp.exp(jax.random.uniform(key_col, (1, D), jnp.float32, math.log(0.3), math.log(3.0)))
    return (base * row_scale * col_scale).astype(jnp.bfloat16)


def draw_expert_ids(key, part):
    key = jax.random.fold_in(key, 11)
    keys = jax.random.split(key, 6)
    blocks = TOKENS // TOK_DEV
    section_count = blocks // GROUP
    half = CAP // 2
    spread = jax.random.randint(keys[0], (section_count, GROUP // 2), 0, half + 1)
    spread = spread.at[:, 0].set(half)
    paired = jnp.stack([half + spread, half - spread], axis=-1).reshape(section_count, GROUP)
    orders = jax.vmap(lambda k: jax.random.permutation(k, GROUP))(jax.random.split(keys[1], section_count))
    counts = jnp.take_along_axis(paired, orders, axis=1).reshape(blocks)
    ranks = jax.vmap(lambda k: jax.random.permutation(k, TOK_DEV))(jax.random.split(keys[2], blocks))
    chosen = ranks < counts[:, None]
    other = jax.random.randint(keys[3], (blocks, TOK_DEV), 1, EXPERTS)
    offset = jax.random.randint(keys[4], (blocks, TOK_DEV), 1, EXPERTS - 1)
    second = 1 + (other - 1 + offset) % (EXPERTS - 1)
    flip = jax.random.randint(keys[5], (blocks, TOK_DEV), 0, 2)
    first_id = jnp.where(chosen & (flip == 0), 0, other)
    last_id = jnp.where(chosen, jnp.where(flip == 1, 0, other), second)
    return jnp.stack([first_id, last_id], axis=-1).reshape(TOKENS, TOP).astype(jnp.int32)


def steps_of(stream_key, dims, cuts, least, high):
    level = 1.0
    for position, shards_of in cuts:
        steps = jax.random.uniform(jax.random.fold_in(jax.random.fold_in(stream_key, 6), position), (shards_of,), jnp.float32, least / len(cuts), high / len(cuts))
        level = level * jnp.repeat(jnp.exp(steps), dims[position] // shards_of).reshape((-1,) + (1,) * (len(dims) - 1 - position))
    return level


def centred(rng, shape, width, reach, shards=(), held_as=jnp.bfloat16):
    factor_of = steps_of(rng, shape, shards, -0.22, 0.18) if shards else 1.0
    entries = jax.random.normal(rng, shape, jnp.float32) * width * factor_of
    return jnp.minimum(jnp.maximum(entries, -reach), reach).astype(held_as)


def setup_inputs(seed: int = 0) -> dict:
    key_list = jax.random.split(jax.random.key(seed), 8)
    hidden_in = draw_hidden_in(jax.random.fold_in(key_list[7], 71), 0)
    norm_gain = jnp.clip(1.0 + 0.18 * jax.random.normal(key_list[1], (SECTIONS, D), jnp.float32), 0.1, 1.9)
    w_gate = centred(key_list[2], (SECTIONS, D, FF_WIN), D ** -0.5, 0.078125, ((0, 8), (2, 16)))
    w_up = centred(key_list[3], (SECTIONS, D, FF_WIN), D ** -0.5, 0.078125, ((0, 8), (2, 16)))
    w_down = centred(key_list[4], (SECTIONS, FF_WIN, D), FF_WIN ** -0.5, 0.0625, ((0, 8), (1, 16)))
    expert_ids = draw_expert_ids(jax.random.fold_in(key_list[7], 71), 0)
    gate_weights = jnp.clip(0.25 + 0.75 * jax.random.uniform(key_list[6], (TOKENS, TOP), jnp.float32) ** steps_of(key_list[6], (TOKENS, TOP), ((0, 128),), -0.2, 0.2), 0.25, 1.0)
    return dict(hidden_in=hidden_in, norm_gain=norm_gain, w_gate=w_gate, w_up=w_up, w_down=w_down, expert_ids=expert_ids, gate_weights=gate_weights)


def rms_scale(values_in, gain):
    values = values_in.astype(jnp.float32)
    mean_sq = lax.optimization_barrier(jnp.mean(values * values, axis=-1, keepdims=True))
    return (values * lax.rsqrt(mean_sq + 1e-05) * gain).astype(jnp.bfloat16)

def expert_rows(normed, gate_matrix, up_matrix, down_matrix):
    gate = jnp.dot(normed, gate_matrix, preferred_element_type=jnp.float32)
    up_values = jnp.dot(normed, up_matrix, preferred_element_type=jnp.float32)
    hidden = (jax.nn.silu(gate) * up_values).astype(jnp.bfloat16)
    return jnp.dot(hidden, down_matrix, preferred_element_type=jnp.float32)

def reference(hidden_in, norm_gain, w_gate, w_up, w_down, expert_ids, gate_weights):
    section_rows = GROUP * TOK_DEV
    routed_count = GROUP * CAP // 2
    inputs = hidden_in.reshape(SECTIONS, section_rows, D)
    id_blocks = expert_ids.reshape(SECTIONS, section_rows, TOP)
    gate_blocks = gate_weights.reshape(SECTIONS, section_rows, TOP)

    def one_section(section_args):
        block, gain, gate_matrix, up_matrix, down_matrix, id_rows, gate_rows = section_args
        normed = rms_scale(block, gain)
        chosen = id_rows == 0
        routed = jnp.any(chosen, axis=1)
        own_weight = lax.optimization_barrier(jnp.sum(jnp.where(chosen, gate_rows, 0.0), axis=1))
        order = jnp.argsort(jnp.where(routed, 0, 1).astype(jnp.int32), stable=True)[:routed_count].astype(jnp.int32)
        result = expert_rows(normed[order], gate_matrix, up_matrix, down_matrix)
        branch = jnp.zeros((section_rows, D), result.dtype).at[order].set(result)
        combined = block.astype(jnp.float32) + own_weight[:, None] * branch
        return combined.astype(jnp.bfloat16)
    outputs = lax.map(one_section, (inputs, norm_gain, w_gate, w_up, w_down, id_blocks, gate_blocks))
    return jnp.roll(outputs, 1, axis=0).reshape(SECTIONS * section_rows, D)
```

```python
import functools

import jax
import jax.numpy as jnp
from jax import lax
from jax.experimental import pallas as pl
from jax.experimental.pallas import tpu as pltpu
from jax.sharding import PartitionSpec as P

MESH = pl.DeviceIdType.MESH
F32 = jnp.float32
BF16 = jnp.bfloat16
CHIPS = 8
MEMBERS = 16


def iota(shape, dim):
    return lax.broadcasted_iota(jnp.int32, shape, dim).astype(F32)


def kernel(
    sections,
    x_hbm, gain, wg_hbm, wu_hbm, wd_hbm, ids, gw,
    out,
    x_v, x_in, route, route_in, counts, wg, wu, wd, packed, slots, pick, place,
    gath, acc_g, acc_u, hid, own, core_out, core_in, opp_out, opp_in,
    near_out, near_in, cross_out, cross_in, back_out, back_in,
    load_sem, cnt_s, cnt_r, a2a_s, a2a_r, gath_s, gath_r, core_s, core_r,
    opp_s, opp_r, near_s, near_r, cross_s, cross_r, back_s, back_r, relay_s, relay_r,
):
    p, c, d = lax.axis_index("pipe"), lax.axis_index("expert"), lax.axis_index("dp")
    y, z = d // 4, d % 4
    me = d * 2 + c
    after, before = lax.rem(p + 1, sections), lax.rem(p + sections - 1, sections)
    tokens, width = x_v.shape
    cap = packed.shape[1]
    part = packed.shape[2]
    half = gath.shape[3]
    rows = 2 * half

    def chip(other_y, step):
        yy = 1 - y if other_y else y
        return yy * 4 + (z + step) % 4

    up, down, across = chip(False, 1), chip(False, 3), chip(True, 0)
    to_up, to_down, to_across = (p, c, up), (p, c, down), (p, c, across)
    to_core = (p, 1 - c, d)

    def remote(src, dst, send, recv, device):
        return pltpu.make_async_remote_copy(
            src_ref=src, dst_ref=dst, send_sem=send, recv_sem=recv,
            device_id=device, device_id_type=MESH,
        )

    load_x = pltpu.make_async_copy(x_hbm, x_v, load_sem.at[0])
    load_g = pltpu.make_async_copy(wg_hbm, wg, load_sem.at[1])
    load_u = pltpu.make_async_copy(wu_hbm, wu, load_sem.at[2])
    load_x.start()

    barrier = pltpu.get_barrier_semaphore()

    def member(i):
        return i % 2, i // 2

    def greet(k, carry):
        e, dd = member((me + k) % MEMBERS)
        pl.semaphore_signal(barrier, inc=1, device_id=(p, e, dd), device_id_type=MESH)
        return carry

    def greet_before(k, carry):
        e, dd = member(k)
        pl.semaphore_signal(barrier, inc=1, device_id=(before, e, dd), device_id_type=MESH)
        return carry

    lax.fori_loop(1, MEMBERS, greet, 0)
    lax.fori_loop(0, MEMBERS, greet_before, 0)

    load_g.start()
    load_u.start()
    loads_d = []
    for e in range(2):
        for j in range(CHIPS):
            cp = pltpu.make_async_copy(
                wd_hbm.at[:, pl.ds((2 * j + e) * part, part)], wd.at[j, e],
                load_sem.at[3 + 2 * j + e],
            )
            cp.start()
            loads_d.append(cp)

    chosen = ids[...] == 0
    routed = jnp.max(jnp.where(chosen, 1.0, 0.0), axis=1, keepdims=True)
    weight = jnp.sum(jnp.where(chosen, gw[...], 0.0), axis=1, keepdims=True)
    routed_b = jnp.broadcast_to(routed, (tokens, tokens))
    tri = jnp.where(iota((tokens, tokens), 0) >= iota((tokens, tokens), 1), 1.0, 0.0)
    rank = jnp.dot(tri.astype(BF16), routed_b.astype(BF16), preferred_element_type=F32)
    lane = iota((tokens, tokens), 1)
    spot = jnp.where((routed_b > 0.5) & (rank - 1.0 == lane), 1.0, 0.0)
    route[...] = jnp.where(lane < cap, spot, jnp.broadcast_to(weight, (tokens, tokens)))
    spot_t = spot.T[:cap].astype(BF16)
    counts[me] = jnp.dot(
        jnp.ones((8, tokens), BF16), routed_b.astype(BF16), preferred_element_type=F32
    )

    load_x.wait()

    def squares(j, total):
        v = x_v[:, pl.ds(pl.multiple_of(j * part, 128), part)].astype(F32)
        return total + jnp.sum(v * v, axis=1, keepdims=True)

    total = lax.fori_loop(0, MEMBERS, squares, jnp.zeros((tokens, 1), F32))
    scale = lax.rsqrt(total / width + 1e-05)

    def pack(j, carry):
        at = pl.ds(pl.multiple_of(j * part, 128), part)
        n = (x_v[:, at].astype(F32) * scale * gain[:, at]).astype(BF16)
        packed[j] = jnp.dot(spot_t, n, preferred_element_type=F32).astype(BF16)
        return carry

    lax.fori_loop(0, MEMBERS, pack, 0)
    slots[me] = packed[me]

    pl.semaphore_wait(barrier, 2 * MEMBERS - 1)

    def count_copy(k):
        i = (me + k) % MEMBERS
        e, dd = member(i)
        return remote(counts.at[me], counts.at[me], cnt_s.at[i], cnt_r.at[me], (p, e, dd))

    def count_from(k):
        i = (me + k) % MEMBERS
        return remote(counts.at[i], counts.at[i], cnt_s.at[i], cnt_r.at[i], to_core)

    def slot_copy(k):
        i = (me + k) % MEMBERS
        e, dd = member(i)
        return remote(packed.at[i], slots.at[me], a2a_s.at[i], a2a_r.at[me], (p, e, dd))

    def slot_from(k):
        i = (me + k) % MEMBERS
        return remote(packed.at[i], slots.at[i], a2a_s.at[i], a2a_r.at[i], to_core)

    def loop(first, last, body):
        def step(k, carry):
            body(k)
            return carry

        lax.fori_loop(first, last, step, 0)

    loop(1, MEMBERS, lambda k: count_copy(k).start())
    loop(1, MEMBERS, lambda k: slot_copy(k).start())
    relay_route = remote(route, route_in, relay_s.at[0], relay_r.at[0], (after, c, d))
    relay_route.start()
    loop(1, MEMBERS, lambda k: count_from(k).wait_recv())

    off = jnp.zeros((1, 128), F32)
    lane1 = iota((1, 128), 1)
    row_i = iota((rows, 128), 0)
    s_i, r_i = iota((cap, rows), 0), iota((cap, rows), 1)
    for q in range(MEMBERS // 2):
        n0, n1 = counts[2 * q][0:1], counts[2 * q + 1][0:1]
        high = lane1 - cap
        target = jnp.where(
            lane1 < cap,
            jnp.where(lane1 < n0, off + lane1, -1.0),
            jnp.where(high < n1, off + n0 + high, -1.0),
        )
        pick[:, q * 128:(q + 1) * 128] = jnp.where(row_i == target, 1.0, 0.0).astype(BF16)
        for t, (o, n) in enumerate(((off, n0), (off + n0, n1))):
            hit = (r_i - s_i == o[:, 0:1]) & (s_i < n[:, 0:1])
            place[(2 * q + t) * cap:(2 * q + t + 1) * cap] = jnp.where(hit, 1.0, 0.0).astype(BF16)
        off = off + n0 + n1

    loop(1, MEMBERS, lambda k: slot_from(k).wait_recv())
    all_slots = slots[...].reshape(MEMBERS * cap, part)
    for h in range(2):
        gath[d, c, h] = jnp.dot(
            pick[h * half:(h + 1) * half], all_slots, preferred_element_type=F32
        ).astype(BF16)

    sends = []

    def piece(j, e, h):
        return gath.at[j, e, h], gath_r.at[j, e, h]

    def send_piece(j, h, device):
        ref, sem = piece(j, c, h)
        cp = remote(ref, ref, gath_s.at[len(sends)], sem, device)
        cp.start()
        sends.append(cp)

    def wait_piece(j, e, h):
        ref, sem = piece(j, e, h)
        remote(ref, ref, gath_s.at[0], sem, to_core).wait_recv()

    def multiply(j, first=False):
        for h in range(2):
            wait_piece(j, 1 - c, h)

        def tile(n):
            at = pl.ds(pl.multiple_of(n * 256, 256), 256)
            a = jnp.concatenate(
                [
                    jnp.concatenate([gath[j, e, h] for e in range(2)], axis=1)
                    for h in range(2)
                ],
                axis=0,
            )
            for w, acc in ((wg, acc_g), (wu, acc_u)):
                v = jnp.dot(a, w[j, :, at], preferred_element_type=F32)
                if first:
                    acc[:, at] = v
                else:
                    acc[:, at] += v

        loop(0, acc_g.shape[1] // 256, tile)

    send_piece(d, 0, to_up)
    send_piece(d, 1, to_down)
    send_piece(d, 0, to_across)
    send_piece(d, 1, to_across)
    send_piece(d, 1, to_up)
    send_piece(d, 0, to_down)
    send_piece(d, 0, to_core)
    send_piece(d, 1, to_core)

    load_g.wait()
    load_u.wait()
    multiply(d, first=True)

    wait_piece(down, c, 0)
    send_piece(down, 0, to_up)
    send_piece(down, 0, to_core)
    wait_piece(up, c, 1)
    send_piece(up, 1, to_down)
    send_piece(up, 1, to_core)
    wait_piece(across, c, 0)
    send_piece(across, 0, to_up)
    send_piece(across, 0, to_core)
    wait_piece(across, c, 1)
    send_piece(across, 1, to_down)
    send_piece(across, 1, to_up)
    send_piece(across, 0, to_down)
    send_piece(across, 1, to_core)
    relay_x = remote(x_v, x_in, relay_s.at[1], relay_r.at[1], (after, c, d))
    relay_x.start()
    wait_piece(down, c, 1)
    send_piece(down, 1, to_core)
    wait_piece(up, c, 0)
    send_piece(up, 0, to_core)
    multiply(across)
    multiply(down)
    multiply(up)
    aup, adown = chip(True, 1), chip(True, 3)
    wait_piece(adown, c, 0)
    send_piece(adown, 0, to_up)
    send_piece(adown, 0, to_core)
    wait_piece(aup, c, 1)
    send_piece(aup, 1, to_down)
    send_piece(aup, 1, to_core)
    wait_piece(adown, c, 1)
    send_piece(adown, 1, to_core)
    wait_piece(aup, c, 0)
    send_piece(aup, 0, to_core)
    far, afar = chip(False, 2), chip(True, 2)
    wait_piece(far, c, 0)
    send_piece(far, 0, to_core)
    wait_piece(far, c, 1)
    send_piece(far, 1, to_core)
    multiply(adown)
    multiply(aup)
    multiply(far)
    wait_piece(afar, c, 0)
    send_piece(afar, 0, to_core)
    wait_piece(afar, c, 1)
    send_piece(afar, 1, to_core)
    multiply(afar)

    def activate(n):
        at = pl.ds(pl.multiple_of(n * 128, 128), 128)
        g = acc_g[at]
        hid[at] = (g / (1.0 + jnp.exp(-g)) * acc_u[at]).astype(BF16)

    loop(0, rows // 128, activate)
    for cp in loads_d:
        cp.wait()

    order = [(o, s) for o in (True, False) for s in (2, 1, 3, 0)]
    core_copies = []

    def project(k):
        j = chip(*order[k])
        a = hid[...]
        core_out[k] = jnp.dot(a, wd[j, 1 - c], preferred_element_type=F32).astype(BF16)
        cp = remote(core_out.at[k], core_in.at[k], core_s.at[k], core_r.at[k], to_core)
        cp.start()
        core_copies.append(cp)
        own[k] = jnp.dot(a, wd[j, c], preferred_element_type=F32)

    def both(k, h):
        at = pl.ds(h * half, half)
        return own[k, at] + core_in[k, at].astype(F32)

    others = []

    def pass_on(src, dst, send, recv, device):
        cp = remote(src, dst, send, recv, device)
        cp.start()
        others.append(cp)

    def send_far(g):
        core_copies[4 * g].wait_recv()
        for h, device in ((0, to_up), (1, to_down)):
            opp_out[g, h] = both(4 * g, h).astype(BF16)
            pass_on(opp_out.at[g, h], opp_in.at[g, h], opp_s.at[g, h], opp_r.at[g, h], device)

    def send_near(g, way, h, add):
        k = 4 * g + 1 + way
        v = both(k, h)
        if add:
            v = v + opp_in[g, h].astype(F32)
        near_out[g, way, h] = v.astype(BF16)
        pass_on(
            near_out.at[g, way, h], near_in.at[g, way, h],
            near_s.at[g, way, h], near_r.at[g, way, h], to_down if way else to_up,
        )

    def wait_far(g, h):
        remote(
            opp_out.at[g, h], opp_in.at[g, h], opp_s.at[g, h], opp_r.at[g, h], to_up
        ).wait_recv()

    def wait_near(g):
        for way in range(2):
            for h in range(2):
                remote(
                    near_out.at[g, way, h], near_in.at[g, way, h],
                    near_s.at[g, way, h], near_r.at[g, way, h], to_up,
                ).wait_recv()

    def collect(g, h):
        return both(4 * g + 3, h) + near_in[g, 0, h].astype(F32) + near_in[g, 1, h].astype(F32)

    def dependent(g):
        wait_far(g, 0)
        send_near(g, 0, 0, True)
        wait_far(g, 1)
        send_near(g, 1, 1, True)

    project(0)
    project(1)
    send_far(0)
    project(2)
    core_copies[1].wait_recv()
    send_near(0, 0, 1, False)
    project(3)
    core_copies[2].wait_recv()
    send_near(0, 1, 0, False)
    project(4)
    project(5)
    dependent(0)
    send_far(1)
    project(6)
    core_copies[5].wait_recv()
    send_near(1, 0, 1, False)
    project(7)
    core_copies[6].wait_recv()
    send_near(1, 1, 0, False)
    dependent(1)
    core_copies[3].wait_recv()
    wait_near(0)
    for h in range(2):
        cross_out[h] = collect(0, h).astype(BF16)
    cross = remote(cross_out, cross_in, cross_s, cross_r, to_across)
    cross.start()
    core_copies[7].wait_recv()
    wait_near(1)
    cross.wait_recv()
    final = jnp.concatenate(
        [(collect(1, h) + cross_in[h].astype(F32)).astype(BF16) for h in range(2)], axis=0
    )

    def unpack(i):
        at = pl.ds(pl.multiple_of(i * cap, cap), cap)
        back_out[i] = jnp.dot(place[at], final, preferred_element_type=F32).astype(BF16)
        e, dd = member(i)
        remote(
            back_out.at[i], back_in.at[me], back_s.at[i], back_r.at[me], (after, e, dd)
        ).start()

    loop(0, MEMBERS, unpack)

    relay_route.wait_recv()
    relay_x.wait_recv()
    spread = route_in[:, :cap].astype(BF16)
    scale_in = route_in[:, cap:cap + 1]

    def back_from(k):
        return remote(back_out.at[k], back_in.at[k], back_s.at[k], back_r.at[k], to_core)

    def finish(k):
        back_from(k).wait_recv()
        at = pl.ds(pl.multiple_of(k * part, 128), part)
        term = jnp.dot(spread, back_in[k], preferred_element_type=F32)
        out[:, at] = (x_in[:, at].astype(F32) + scale_in * term).astype(BF16)

    loop(0, MEMBERS, finish)

    loop(1, MEMBERS, lambda k: count_copy(k).wait_send())
    loop(1, MEMBERS, lambda k: slot_copy(k).wait_send())
    loop(0, MEMBERS, lambda k: back_from(k).wait_send())
    for cp in sends + core_copies + others + [cross, relay_route, relay_x]:
        cp.wait_send()


def solution(mesh):
    sections = mesh.shape["pipe"]

    def per_device(hidden_in, norm_gain, w_gate, w_up, w_down, expert_ids, gate_weights):
        tokens, width = hidden_in.shape
        ff = w_gate.shape[2]
        cap = tokens // 2
        rows = MEMBERS * cap // 2
        half = rows // 2
        part = width // MEMBERS
        vmem = pltpu.VMEM
        dma = pltpu.SemaphoreType.DMA
        any_space = pl.BlockSpec(memory_space=pl.ANY)
        in_vmem = pl.BlockSpec(memory_space=pltpu.VMEM)
        return pl.pallas_call(
            functools.partial(kernel, sections),
            out_shape=jax.ShapeDtypeStruct((tokens, width), BF16),
            in_specs=[any_space, in_vmem, any_space, any_space, any_space, in_vmem, in_vmem],
            out_specs=in_vmem,
            scratch_shapes=[
                vmem((tokens, width), BF16),
                vmem((tokens, width), BF16),
                vmem((tokens, tokens), F32),
                vmem((tokens, tokens), F32),
                vmem((MEMBERS, 8, 128), F32),
                vmem((CHIPS, 2 * part, ff), BF16),
                vmem((CHIPS, 2 * part, ff), BF16),
                vmem((CHIPS, 2, ff, part), BF16),
                vmem((MEMBERS, cap, part), BF16),
                vmem((MEMBERS, cap, part), BF16),
                vmem((rows, MEMBERS * cap), BF16),
                vmem((MEMBERS * cap, rows), BF16),
                vmem((CHIPS, 2, 2, half, part), BF16),
                vmem((rows, ff), F32),
                vmem((rows, ff), F32),
                vmem((rows, ff), BF16),
                vmem((CHIPS, rows, part), F32),
                vmem((CHIPS, rows, part), BF16),
                vmem((CHIPS, rows, part), BF16),
                vmem((2, 2, half, part), BF16),
                vmem((2, 2, half, part), BF16),
                vmem((2, 2, 2, half, part), BF16),
                vmem((2, 2, 2, half, part), BF16),
                vmem((2, half, part), BF16),
                vmem((2, half, part), BF16),
                vmem((MEMBERS, cap, part), BF16),
                vmem((MEMBERS, cap, part), BF16),
                dma((19,)),
                dma((MEMBERS,)), dma((MEMBERS,)),
                dma((MEMBERS,)), dma((MEMBERS,)),
                dma((32,)), dma((CHIPS, 2, 2)),
                dma((CHIPS,)), dma((CHIPS,)),
                dma((2, 2)), dma((2, 2)),
                dma((2, 2, 2)), dma((2, 2, 2)),
                dma, dma,
                dma((MEMBERS,)), dma((MEMBERS,)),
                dma((2,)), dma((2,)),
            ],
            compiler_params=pltpu.CompilerParams(
                collective_id=0, has_side_effects=True, vmem_limit_bytes=62 * 2**20
            ),
            name="routed_block",
        )(
            hidden_in,
            norm_gain,
            w_gate.reshape(CHIPS, 2 * part, ff),
            w_up.reshape(CHIPS, 2 * part, ff),
            w_down.reshape(ff, width),
            expert_ids,
            gate_weights,
        )

    return jax.shard_map(
        per_device,
        mesh=mesh,
        in_specs=(
            P(("pipe", "expert", "dp"), None),
            P("pipe", None),
            P("pipe", None, ("expert", "dp")),
            P("pipe", None, ("expert", "dp")),
            P("pipe", ("expert", "dp"), None),
            P(("pipe", "expert", "dp"), None),
            P(("pipe", "expert", "dp"), None),
        ),
        out_specs=P(("pipe", "expert", "dp"), None),
        check_vma=False,
    )
```

```python
import functools

import jax
import jax.numpy as jnp
from jax import lax
from jax.experimental import pallas as pl
from jax.experimental.pallas import tpu as pltpu
from jax.sharding import PartitionSpec as P

MESH = pl.DeviceIdType.MESH
F32 = jnp.float32
BF16 = jnp.bfloat16
CHIPS = 8
MEMBERS = 16
LANES = 128


def iota(shape, dim):
    return lax.broadcasted_iota(jnp.int32, shape, dim).astype(F32)


def kernel(
    sections,
    x_hbm, gain, wg_hbm, wu_hbm, wd_hbm, ids, gw,
    out,
    x_v, x_in, route, route_in, counts, counts_in, wg, wu, wd, packed, slots, pick, place,
    gath, acc_g, acc_u, hid, own, core_out, core_in, opp_out, opp_in,
    near_out, near_in, sum_out, sum_in, back_out, back_in,
    load_sem, cnt_s, cnt_r, a2a_s, a2a_r, gath_s, gath_r, core_s, core_r,
    opp_s, opp_r, near_s, near_r, sum_s, sum_r, back_s, back_r, relay_s, relay_r,
):
    p, c, d = lax.axis_index("pipe"), lax.axis_index("expert"), lax.axis_index("dp")
    y, z = d // 4, d % 4
    me = d * 2 + c
    after, before = lax.rem(p + 1, sections), lax.rem(p + sections - 1, sections)
    tokens, width = x_v.shape
    cap = packed.shape[1]
    part = packed.shape[2]
    half = gath.shape[3]
    rows = 2 * half
    strips = part // LANES
    cuts = ((0, LANES), (LANES, part - LANES))

    def chip(other_y, step):
        yy = 1 - y if other_y else y
        return yy * 4 + (z + step) % 4

    up, down, across = chip(False, 1), chip(False, 3), chip(True, 0)
    to_up, to_down, to_across = (p, c, up), (p, c, down), (p, c, across)
    to_core = (p, 1 - c, d)

    def remote(src, dst, send, recv, device):
        return pltpu.make_async_remote_copy(
            src_ref=src, dst_ref=dst, send_sem=send, recv_sem=recv,
            device_id=device, device_id_type=MESH,
        )

    def loop(first, last, body):
        def step(k, carry):
            body(k)
            return carry

        lax.fori_loop(first, last, step, 0)

    def member(k):
        i = (me + k) % MEMBERS
        return i, (p, i % 2, i // 2)

    load_x = pltpu.make_async_copy(x_hbm, x_v, load_sem.at[0])
    load_g = pltpu.make_async_copy(wg_hbm, wg, load_sem.at[1])
    load_u = pltpu.make_async_copy(wu_hbm, wu, load_sem.at[2])
    load_x.start()

    barrier = pltpu.get_barrier_semaphore()

    def greet(device):
        pl.semaphore_signal(barrier, inc=1, device_id=device, device_id_type=MESH)

    loop(1, MEMBERS, lambda k: greet(member(k)[1]))
    greet((before, c, d))
    greet((before, c, across))

    square = (tokens, tokens)
    chosen = ids[...] == 0
    routed = jnp.max(jnp.where(chosen, 1.0, 0.0), axis=0, keepdims=True)
    weight = jnp.sum(jnp.where(chosen, gw[...], 0.0), axis=0, keepdims=True)
    routed_b = jnp.broadcast_to(routed, square)
    tri = jnp.where(iota(square, 0) <= iota(square, 1), 1.0, 0.0).astype(BF16)
    rank = jnp.dot(routed_b.astype(BF16), tri, preferred_element_type=F32)
    spot = jnp.where((routed_b > 0.5) & (rank - 1.0 == iota(square, 0)), 1.0, 0.0)
    spot_t = spot[:cap].astype(BF16)
    route[...] = jnp.where(
        iota(square, 1) < cap, spot.T, jnp.broadcast_to(weight, square).T
    )
    counts[me] = jnp.dot(
        routed_b[:8].astype(BF16), jnp.ones(square, BF16), preferred_element_type=F32
    )

    load_x.wait()
    load_g.start()
    load_u.start()
    loads_d = []
    for j in range(CHIPS):
        for e in range(2):
            cp = pltpu.make_async_copy(
                wd_hbm.at[:, pl.ds((2 * j + e) * part, part)], wd.at[j, e],
                load_sem.at[3 + 2 * j + e],
            )
            cp.start()
            loads_d.append(cp)

    def squares(j, total):
        for t in range(strips):
            at = pl.ds(pl.multiple_of(j * part + t * LANES, LANES), LANES)
            v = x_v[:, at].astype(F32)
            total = total + v * v
        return total

    total = lax.fori_loop(0, MEMBERS, squares, jnp.zeros((tokens, LANES), F32))
    scale = lax.rsqrt(jnp.sum(total, axis=1, keepdims=True) / width + 1e-05)

    def pack(j, q):
        start, size = cuts[q]
        for t in range(4):
            i = j * 4 + t
            at = pl.ds(pl.multiple_of(i * part + start, LANES), size)
            n = (x_v[:, at].astype(F32) * scale * gain[:, at]).astype(BF16)
            packed[i, :, start:start + size] = jnp.dot(
                spot_t, n, preferred_element_type=F32
            ).astype(BF16)

    loop(0, MEMBERS // 4, lambda j: pack(j, 0))
    pl.semaphore_wait(barrier, MEMBERS + 1)

    def count_copy(k):
        i, device = member(k)
        return remote(counts.at[me], counts.at[me], cnt_s.at[i], cnt_r.at[me], device)

    def count_from(k):
        i = member(k)[0]
        return remote(counts.at[i], counts.at[i], cnt_s.at[i], cnt_r.at[i], to_core)

    def slot_copy(k, q):
        i, device = member(k)
        at = pl.ds(*cuts[q])
        return remote(
            packed.at[i, :, at], slots.at[me, :, at], a2a_s.at[q, i], a2a_r.at[q, me], device
        )

    def slot_from(k, q):
        i = member(k)[0]
        at = pl.ds(*cuts[q])
        return remote(
            packed.at[i, :, at], slots.at[i, :, at], a2a_s.at[q, i], a2a_r.at[q, i], to_core
        )

    loop(1, MEMBERS, lambda k: count_copy(k).start())

    loop(1, MEMBERS, lambda k: slot_copy(k, 0).start())
    loop(0, MEMBERS // 4, lambda j: pack(j, 1))
    loop(1, MEMBERS, lambda k: slot_copy(k, 1).start())
    slots[me] = packed[me]
    loop(1, MEMBERS, lambda k: count_from(k).wait_recv())
    counterpart = (after, c, d)
    relay_route = remote(route, route_in, relay_s.at[0], relay_r.at[0], counterpart)
    relay_route.start()
    relay_counts = remote(counts, counts_in, relay_s.at[1], relay_r.at[1], counterpart)
    relay_counts.start()

    off = jnp.zeros((1, LANES), F32)
    lane1 = iota((1, LANES), 1)
    high = lane1 - cap
    row_i = iota((rows, LANES), 0)
    for q in range(MEMBERS // 2):
        n0, n1 = counts[2 * q][0:1], counts[2 * q + 1][0:1]
        target = jnp.where(
            lane1 < cap,
            jnp.where(lane1 < n0, off + lane1, -1.0),
            jnp.where(high < n1, off + n0 + high, -1.0),
        )
        pick[:, q * LANES:(q + 1) * LANES] = jnp.where(row_i == target, 1.0, 0.0).astype(BF16)
        off = off + n0 + n1

    sends = []

    def piece(j, e, h, q):
        return gath.at[j, e, h, :, pl.ds(*cuts[q])], gath_r.at[j, e, h, q]

    def send_piece(j, h, q, device):
        ref, sem = piece(j, c, h, q)
        cp = remote(ref, ref, gath_s.at[len(sends)], sem, device)
        cp.start()
        sends.append(cp)

    def wait_piece(j, e, h, q):
        ref, sem = piece(j, e, h, q)
        remote(ref, ref, gath_s.at[0], sem, to_core).wait_recv()

    def multiply(j, q, first=False):
        start, size = cuts[q]
        for h in range(2):
            wait_piece(j, 1 - c, h, q)

        def tile(n):
            at = pl.ds(pl.multiple_of(n * 256, 256), 256)
            cols = slice(start, start + size)
            a = jnp.concatenate(
                [
                    jnp.concatenate([gath[j, e, h, :, cols] for e in range(2)], axis=1)
                    for h in range(2)
                ],
                axis=0,
            )
            for w, acc in ((wg, acc_g), (wu, acc_u)):
                b = jnp.concatenate([w[j, e, cols, at] for e in range(2)], axis=0)
                v = jnp.dot(a, b, preferred_element_type=F32)
                if first:
                    acc[:, at] = v
                else:
                    acc[:, at] += v

        loop(0, acc_g.shape[1] // 256, tile)

    def to_z(j, q, first):
        if first:
            send_piece(j, 0, q, to_up)
            send_piece(j, 1, q, to_down)
        else:
            send_piece(j, 1, q, to_up)
            send_piece(j, 0, q, to_down)

    def forward(below, above, q):
        wait_piece(below, c, 0, q)
        send_piece(below, 0, q, to_up)
        send_piece(below, 0, q, to_core)
        wait_piece(above, c, 1, q)
        send_piece(above, 1, q, to_down)
        send_piece(above, 1, q, to_core)

    def rest(below, above, q):
        wait_piece(below, c, 1, q)
        send_piece(below, 1, q, to_core)
        wait_piece(above, c, 0, q)
        send_piece(above, 0, q, to_core)

    def from_across(q):
        for h in range(2):
            wait_piece(across, c, h, q)
        to_z(across, q, True)
        to_z(across, q, False)
        for h in range(2):
            send_piece(across, h, q, to_core)

    def from_far(j, q):
        for h in range(2):
            wait_piece(j, c, h, q)
            send_piece(j, h, q, to_core)

    for q, (start, size) in enumerate(cuts):
        loop(1, MEMBERS, lambda k: slot_from(k, q).wait_recv())
        all_slots = slots[:, :, start:start + size].reshape(MEMBERS * cap, size)
        for h in range(2):
            gath[d, c, h, :, start:start + size] = jnp.dot(
                pick[h * half:(h + 1) * half], all_slots, preferred_element_type=F32
            ).astype(BF16)
        to_z(d, q, True)
        send_piece(d, 0, q, to_across)
        send_piece(d, 1, q, to_across)
        to_z(d, q, False)
        send_piece(d, 0, q, to_core)
        send_piece(d, 1, q, to_core)

    aup, adown, far, afar = chip(True, 1), chip(True, 3), chip(False, 2), chip(True, 2)
    load_g.wait()
    load_u.wait()
    multiply(d, 0, first=True)
    forward(down, up, 0)
    from_across(0)
    rest(down, up, 0)

    relay_counts.wait_recv()
    off = jnp.zeros((1, LANES), F32)
    s_i, r_i = iota((cap, rows), 0), iota((cap, rows), 1)
    for i in range(MEMBERS):
        n = counts_in[i][0:1]
        hit = (r_i - s_i == off[:, 0:1]) & (s_i < n[:, 0:1])
        place[i * cap:(i + 1) * cap] = jnp.where(hit, 1.0, 0.0).astype(BF16)
        off = off + n

    multiply(d, 1)
    multiply(across, 0)
    forward(down, up, 1)
    multiply(down, 0)
    multiply(up, 0)
    from_across(1)
    relay_x = remote(x_v, x_in, relay_s.at[2], relay_r.at[2], counterpart)
    relay_x.start()
    loop(1, MEMBERS, lambda k: count_copy(k).wait_send())
    for q in range(2):
        loop(1, MEMBERS, lambda k: slot_copy(k, q).wait_send())
    forward(adown, aup, 0)
    multiply(across, 1)
    rest(adown, aup, 0)
    rest(down, up, 1)
    multiply(down, 1)
    multiply(up, 1)
    multiply(adown, 0)
    multiply(aup, 0)
    from_far(far, 0)
    forward(adown, aup, 1)
    from_far(far, 1)
    multiply(far, 0)
    multiply(far, 1)
    rest(adown, aup, 1)
    from_far(afar, 0)
    multiply(adown, 1)
    multiply(aup, 1)
    multiply(afar, 0)
    from_far(afar, 1)
    multiply(afar, 1)

    def activate(n):
        at = pl.ds(pl.multiple_of(n * 128, 128), 128)
        g = acc_g[at]
        hid[at] = (g / (1.0 + jnp.exp(-g)) * acc_u[at]).astype(BF16)

    loop(0, rows // 128, activate)
    for cp in loads_d:
        cp.wait()

    order = [(o, s) for o in (True, False) for s in (2, 1, 3, 0)]
    core_copies = {}
    others = []

    def project(q, k):
        j = chip(*order[k])
        cols = slice(q * LANES, (q + 1) * LANES)
        w = jnp.concatenate([wd[j, 1 - c, :, cols], wd[j, c, :, cols]], axis=1)
        v = jnp.dot(hid[...], w, preferred_element_type=F32)
        core_out[q, k] = v[:, :LANES].astype(BF16)
        cp = remote(
            core_out.at[q, k], core_in.at[q, k], core_s.at[q, k], core_r.at[q, k], to_core
        )
        cp.start()
        core_copies[q, k] = cp
        own[q, k] = v[:, LANES:]

    def both(q, k, h):
        at = pl.ds(h * half, half)
        return own[q, k, at] + core_in[q, k, at].astype(F32)

    def pass_on(src, dst, send, recv, device):
        cp = remote(src, dst, send, recv, device)
        cp.start()
        others.append(cp)

    def send_far(q, g):
        core_copies[q, 4 * g].wait_recv()
        for h, device in ((0, to_up), (1, to_down)):
            opp_out[q, g, h] = both(q, 4 * g, h).astype(BF16)
            pass_on(
                opp_out.at[q, g, h], opp_in.at[q, g, h],
                opp_s.at[q, g, h], opp_r.at[q, g, h], device,
            )

    def send_near(q, g, way, h, add):
        v = both(q, 4 * g + 1 + way, h)
        if add:
            v = v + opp_in[q, g, h].astype(F32)
        near_out[q, g, way, h] = v.astype(BF16)
        pass_on(
            near_out.at[q, g, way, h], near_in.at[q, g, way, h],
            near_s.at[q, g, way, h], near_r.at[q, g, way, h], to_down if way else to_up,
        )

    def free_near(q, g):
        for way, h in ((0, 1), (1, 0)):
            core_copies[q, 4 * g + 1 + way].wait_recv()
            send_near(q, g, way, h, False)

    def independent(q):
        for g in range(2):
            send_far(q, g)
        for g in range(2):
            free_near(q, g)

    def dependent(q):
        for g in range(2):
            for way, h in ((0, 0), (1, 1)):
                remote(
                    opp_out.at[q, g, h], opp_in.at[q, g, h],
                    opp_s.at[q, g, h], opp_r.at[q, g, h], to_up,
                ).wait_recv()
                send_near(q, g, way, h, True)

    def collect(q):
        for g in range(2):
            core_copies[q, 4 * g + 3].wait_recv()
            for way in range(2):
                for h in range(2):
                    remote(
                        near_out.at[q, g, way, h], near_in.at[q, g, way, h],
                        near_s.at[q, g, way, h], near_r.at[q, g, way, h], to_up,
                    ).wait_recv()
            for h in range(2):
                sum_out[q, g, h * half:(h + 1) * half] = (
                    both(q, 4 * g + 3, h)
                    + near_in[q, g, 0, h].astype(F32)
                    + near_in[q, g, 1, h].astype(F32)
                ).astype(BF16)
            pass_on(
                sum_out.at[q, g], sum_in.at[q, y], sum_s.at[q, g], sum_r.at[q, y],
                (after, c, d if g else across),
            )

    def back_copy(k, q):
        i, device = member(k)
        return remote(
            back_out.at[q, i], back_in.at[q, me], back_s.at[q, i], back_r.at[q, me], device
        )

    def back_from(k, q):
        i = member(k)[0]
        return remote(
            back_out.at[q, i], back_in.at[q, i], back_s.at[q, i], back_r.at[q, i], to_core
        )

    def unpack(q):
        for t in range(2):
            remote(
                sum_out.at[q, t], sum_in.at[q, t], sum_s.at[q, t], sum_r.at[q, t], to_core
            ).wait_recv()
        final = (sum_in[q, 0].astype(F32) + sum_in[q, 1].astype(F32)).astype(BF16)
        back_out[q] = (
            jnp.dot(place[...], final, preferred_element_type=F32)
            .astype(BF16)
            .reshape(MEMBERS, cap, LANES)
        )
        loop(1, MEMBERS, lambda k: back_copy(k, q).start())
        back_in[q, me] = back_out[q, me]

    def finish(q):
        spread = route_in[:, :cap].astype(BF16)
        scale_in = route_in[:, cap:cap + 1]
        loop(1, MEMBERS, lambda k: back_from(k, q).wait_recv())

        for k in range(0, MEMBERS, 2):
            pair = jnp.concatenate([back_in[q, k], back_in[q, k + 1]], axis=1)
            term = scale_in * jnp.dot(spread, pair, preferred_element_type=F32)
            for t in range(2):
                start = (k + t) * part + q * LANES
                at = slice(start, start + LANES)
                v = x_in[:, at].astype(F32) + term[:, t * LANES:(t + 1) * LANES]
                out[:, at] = v.astype(BF16)

    def projects(q):
        for k in (0, 4, 1, 2, 5, 6, 3, 7):
            project(q, k)

    project(0, 0)
    project(0, 4)
    project(0, 1)
    project(0, 2)
    send_far(0, 0)
    project(0, 5)
    send_far(0, 1)
    project(0, 6)
    free_near(0, 0)
    project(0, 3)
    project(0, 7)
    free_near(0, 1)
    projects(1)
    dependent(0)
    independent(1)
    projects(2)
    collect(0)
    dependent(1)
    independent(2)
    collect(1)
    dependent(2)
    unpack(0)
    collect(2)
    unpack(1)
    relay_route.wait_recv()
    relay_x.wait_recv()
    finish(0)
    unpack(2)
    finish(1)
    for cp in sends + list(core_copies.values()) + others:
        cp.wait_send()
    for cp in (relay_route, relay_counts, relay_x):
        cp.wait_send()
    for q in range(2):
        loop(1, MEMBERS, lambda k: back_copy(k, q).wait_send())
    finish(2)
    loop(1, MEMBERS, lambda k: back_copy(k, 2).wait_send())


def solution(mesh):
    sections = mesh.shape["pipe"]

    def per_device(hidden_in, norm_gain, w_gate, w_up, w_down, expert_ids, gate_weights):
        tokens, width = hidden_in.shape
        ff = w_gate.shape[2]
        cap = tokens // 2
        rows = MEMBERS * cap // 2
        half = rows // 2
        part = width // MEMBERS
        strips = part // LANES
        vmem = pltpu.VMEM
        dma = pltpu.SemaphoreType.DMA
        any_space = pl.BlockSpec(memory_space=pl.ANY)
        in_vmem = pl.BlockSpec(memory_space=pltpu.VMEM)
        return pl.pallas_call(
            functools.partial(kernel, sections),
            out_shape=jax.ShapeDtypeStruct((tokens, width), BF16),
            in_specs=[any_space, in_vmem, any_space, any_space, any_space, in_vmem, in_vmem],
            out_specs=in_vmem,
            scratch_shapes=[
                vmem((tokens, width), BF16),
                vmem((tokens, width), BF16),
                vmem((tokens, tokens), F32),
                vmem((tokens, tokens), F32),
                vmem((MEMBERS, 8, LANES), F32),
                vmem((MEMBERS, 8, LANES), F32),
                vmem((CHIPS, 2, part, ff), BF16),
                vmem((CHIPS, 2, part, ff), BF16),
                vmem((CHIPS, 2, ff, part), BF16),
                vmem((MEMBERS, cap, part), BF16),
                vmem((MEMBERS, cap, part), BF16),
                vmem((rows, MEMBERS * cap), BF16),
                vmem((MEMBERS * cap, rows), BF16),
                vmem((CHIPS, 2, 2, half, part), BF16),
                vmem((rows, ff), F32),
                vmem((rows, ff), F32),
                vmem((rows, ff), BF16),
                vmem((strips, CHIPS, rows, LANES), F32),
                vmem((strips, CHIPS, rows, LANES), BF16),
                vmem((strips, CHIPS, rows, LANES), BF16),
                vmem((strips, 2, 2, half, LANES), BF16),
                vmem((strips, 2, 2, half, LANES), BF16),
                vmem((strips, 2, 2, 2, half, LANES), BF16),
                vmem((strips, 2, 2, 2, half, LANES), BF16),
                vmem((strips, 2, rows, LANES), BF16),
                vmem((strips, 2, rows, LANES), BF16),
                vmem((strips, MEMBERS, cap, LANES), BF16),
                vmem((strips, MEMBERS, cap, LANES), BF16),
                dma((19,)),
                dma((MEMBERS,)), dma((MEMBERS,)),
                dma((2, MEMBERS)), dma((2, MEMBERS)),
                dma((60,)), dma((CHIPS, 2, 2, 2)),
                dma((strips, CHIPS)), dma((strips, CHIPS)),
                dma((strips, 2, 2)), dma((strips, 2, 2)),
                dma((strips, 2, 2, 2)), dma((strips, 2, 2, 2)),
                dma((strips, 2)), dma((strips, 2)),
                dma((strips, MEMBERS)), dma((strips, MEMBERS)),
                dma((3,)), dma((3,)),
            ],
            compiler_params=pltpu.CompilerParams(
                collective_id=0, has_side_effects=True, vmem_limit_bytes=62 * 2**20
            ),
            name="routed_block",
        )(
            hidden_in,
            norm_gain,
            w_gate.reshape(CHIPS, 2, part, ff),
            w_up.reshape(CHIPS, 2, part, ff),
            w_down.reshape(ff, width),
            expert_ids.T,
            gate_weights.T,
        )

    return jax.shard_map(
        per_device,
        mesh=mesh,
        in_specs=(
            P(("pipe", "expert", "dp"), None),
            P("pipe", None),
            P("pipe", None, ("expert", "dp")),
            P("pipe", None, ("expert", "dp")),
            P("pipe", ("expert", "dp"), None),
            P(("pipe", "expert", "dp"), None),
            P(("pipe", "expert", "dp"), None),
        ),
        out_specs=P(("pipe", "expert", "dp"), None),
        check_vma=False,
    )
```

```python
import functools

import jax
import jax.numpy as jnp
from jax import lax
from jax.experimental import pallas as pl
from jax.experimental.pallas import tpu as pltpu
from jax.sharding import PartitionSpec as P

MESH = pl.DeviceIdType.MESH
F32 = jnp.float32
BF16 = jnp.bfloat16
CHIPS = 8
MEMBERS = 16
LANES = 128
TILE = 16


def iota(shape, dim):
    return lax.broadcasted_iota(jnp.int32, shape, dim).astype(F32)


def kernel(
    sections,
    x_hbm, gain_hbm, wg_hbm, wu_hbm, wd_hbm, ids_hbm, gw_hbm,
    out_hbm,
    x_v, x_in, out, gain, ids, gw, route, route_in, counts, counts_in, wg, wu, wd,
    packed_0, packed_1, slots_0, slots_1, pick, place, gath_0, gath_1, acc_g, acc_u, hid, own, core_out, core_in, opp_out, opp_in,
    near_out, near_in, sum_out, sum_in, back_out, back_in,
    load_sem, out_sem, a2a_s, a2a_r, gath_s, gath_r, pair_r, core_s, core_r,
    opp_s, opp_r, near_s, near_r, sum_s, sum_r, back_s, back_r, relay_s, relay_r,
):
    p, c, d = lax.axis_index("pipe"), lax.axis_index("expert"), lax.axis_index("dp")
    y, z = d // 4, d % 4
    me = d * 2 + c
    after, before = lax.rem(p + 1, sections), lax.rem(p + sections - 1, sections)
    tokens, width = x_v.shape
    packed, slots, gath = (packed_0, packed_1), (slots_0, slots_1), (gath_0, gath_1)
    cap = packed_1.shape[1]
    part = LANES + packed_1.shape[2]
    half = gath_0.shape[1]
    rows = 2 * half
    strips = part // LANES
    cuts = ((0, LANES), (LANES, part - LANES))

    def chip(other_y, step):
        yy = 1 - y if other_y else y
        return yy * 4 + (z + step) % 4

    up, down, across = chip(False, 1), chip(False, 3), chip(True, 0)
    to_up, to_down, to_across = (p, c, up), (p, c, down), (p, c, across)
    to_core = (p, 1 - c, d)

    def remote(src, dst, send, recv, device):
        return pltpu.make_async_remote_copy(
            src_ref=src, dst_ref=dst, send_sem=send, recv_sem=recv,
            device_id=device, device_id_type=MESH,
        )

    def loop(first, last, body):
        def step(k, carry):
            body(k)
            return carry

        lax.fori_loop(first, last, step, 0)

    def member(k):
        dd = (y + k // 8) % 2 * 4 + (z + k // 2) % 4
        e = (c + k) % 2
        return dd * 2 + e, (p, e, dd)

    load_x = pltpu.make_async_copy(x_hbm, x_v, load_sem.at[0])
    load_g = pltpu.make_async_copy(wg_hbm, wg, load_sem.at[1])
    load_u = pltpu.make_async_copy(wu_hbm, wu, load_sem.at[2])
    small = [
        pltpu.make_async_copy(src, dst, load_sem.at[4 + n])
        for n, (src, dst) in enumerate(((ids_hbm, ids), (gw_hbm, gw), (gain_hbm, gain)))
    ]
    small[0].start()
    small[1].start()
    load_x.start()
    small[2].start()

    barrier = pltpu.get_barrier_semaphore()

    def greet(device):
        pl.semaphore_signal(barrier, inc=1, device_id=device, device_id_type=MESH)

    loop(1, MEMBERS, lambda k: greet(member(k)[1]))
    greet((before, c, d))
    greet((before, c, across))

    small[0].wait()
    small[1].wait()
    square = (tokens, tokens)
    chosen = ids[...] == 0
    routed = jnp.max(jnp.where(chosen, 1.0, 0.0), axis=0, keepdims=True)
    weight = jnp.sum(jnp.where(chosen, gw[...], 0.0), axis=0, keepdims=True)
    routed_b = jnp.broadcast_to(routed, square)
    tri = jnp.where(iota(square, 0) <= iota(square, 1), 1.0, 0.0).astype(BF16)
    rank = jnp.dot(routed_b.astype(BF16), tri, preferred_element_type=F32)
    spot = jnp.where((routed_b > 0.5) & (rank - 1.0 == iota(square, 0)), 1.0, 0.0)
    spot_t = spot[:cap].astype(BF16)
    route[...] = jnp.where(
        iota(square, 1) < cap, spot.T, jnp.broadcast_to(weight, square).T
    )
    count = jnp.dot(
        routed_b[:TILE].astype(BF16), jnp.ones(square, BF16), preferred_element_type=F32
    ).astype(BF16)
    for i in range(MEMBERS):
        packed_0[i, cap:] = count

    load_x.wait()
    small[2].wait()
    load_g.start()
    load_u.start()
    for j in range(CHIPS):
        for e in range(2):
            pltpu.make_async_copy(
                wd_hbm.at[:, pl.ds((2 * j + e) * part, part)], wd.at[j, e], load_sem.at[3]
            ).start()

    def squares(j, total):
        for t in range(strips):
            at = pl.ds(pl.multiple_of(j * part + t * LANES, LANES), LANES)
            v = x_v[:, at].astype(F32)
            total = total + v * v
        return total

    total = lax.fori_loop(0, MEMBERS, squares, jnp.zeros((tokens, LANES), F32))
    scale = lax.rsqrt(jnp.sum(total, axis=1, keepdims=True) / width + 1e-05)

    def pack(j, q):
        start, size = cuts[q]
        for t in range(4):
            i = j * 4 + t
            at = pl.ds(pl.multiple_of(i * part + start, LANES), size)
            n = (x_v[:, at].astype(F32) * scale * gain[:, at]).astype(BF16)
            packed[q][i, :cap] = jnp.dot(
                spot_t, n, preferred_element_type=F32
            ).astype(BF16)

    loop(0, MEMBERS // 4, lambda j: pack(j, 0))
    pl.semaphore_wait(barrier, MEMBERS + 1)

    def slot_copy(k, q):
        i, device = member(k)
        return remote(
            packed[q].at[i], slots[q].at[me], a2a_s.at[q], a2a_r.at[q], device
        )

    def all_slot_copies(q):
        block = pl.ds(0, MEMBERS - 1)
        return remote(
            packed[q].at[block], slots[q].at[block], a2a_s.at[q], a2a_r.at[q], to_core
        )

    loop(1, MEMBERS, lambda k: slot_copy(MEMBERS - k, 0).start())
    loop(0, MEMBERS // 4, lambda j: pack(j, 1))
    loop(1, MEMBERS, lambda k: slot_copy(MEMBERS - k, 1).start())
    for q in range(2):
        slots[q][me] = packed[q][me]
    all_slot_copies(0).wait_recv()
    counts[...] = slots_0[:, cap:]
    counterpart = (after, c, d)
    relay_route = remote(route, route_in, relay_s.at[0], relay_r.at[0], counterpart)
    relay_route.start()
    relay_counts = remote(counts, counts_in, relay_s.at[1], relay_r.at[1], counterpart)
    relay_counts.start()

    off = jnp.zeros((1, LANES), F32)
    lane1 = iota((1, LANES), 1)
    high = lane1 - cap
    row_i = iota((rows, LANES), 0)
    for q in range(MEMBERS // 2):
        n0, n1 = counts[2 * q].astype(F32)[0:1], counts[2 * q + 1].astype(F32)[0:1]
        target = jnp.where(
            lane1 < cap,
            jnp.where(lane1 < n0, off + lane1, -1.0),
            jnp.where(high < n1, off + n0 + high, -1.0),
        )
        pick[:, q * LANES:(q + 1) * LANES] = jnp.where(row_i == target, 1.0, 0.0).astype(BF16)
        off = off + n0 + n1

    sends = [0, 0]

    def spot_of(j, e, h):
        return (j * 2 + e) * 2 + h

    def send_piece(j, h, q, device):
        ref = gath[q].at[spot_of(j, c, h)]
        if device is to_core:
            sem = pair_r.at[q, j]
        else:
            sem = gath_r.at[q, j, h]
        remote(ref, ref, gath_s.at[q], sem, device).start()
        sends[q] += 1

    def wait_piece(j, h, q):
        ref = gath[q].at[spot_of(j, c, h)]
        remote(ref, ref, gath_s.at[q], gath_r.at[q, j, h], to_core).wait_recv()

    def wait_pair(j, q):
        ref = gath[q].at[pl.ds(spot_of(j, 1 - c, 0), 2)]
        remote(ref, ref, gath_s.at[q], pair_r.at[q, j], to_core).wait_recv()

    def gather_sent(q):
        ref = gath[q].at[pl.ds(0, sends[q])]
        remote(ref, ref, gath_s.at[q], gath_r.at[q, 0, 0], to_core).wait_send()

    def multiply(j, q, first=False):
        start, size = cuts[q]
        wait_pair(j, q)

        def tile(n):
            at = pl.ds(pl.multiple_of(n * 256, 256), 256)
            cols = slice(start, start + size)
            a = jnp.concatenate(
                [
                    jnp.concatenate([gath[q][spot_of(j, e, h)] for e in range(2)], axis=1)
                    for h in range(2)
                ],
                axis=0,
            )
            for w, acc in ((wg, acc_g), (wu, acc_u)):
                b = jnp.concatenate([w[j, e, cols, at] for e in range(2)], axis=0)
                v = jnp.dot(a, b, preferred_element_type=F32)
                if first:
                    acc[:, at] = v
                else:
                    acc[:, at] += v

        loop(0, acc_g.shape[1] // 256, tile)

    def to_z(j, q, first):
        if first:
            send_piece(j, 0, q, to_up)
            send_piece(j, 1, q, to_down)
        else:
            send_piece(j, 1, q, to_up)
            send_piece(j, 0, q, to_down)

    def forward(below, above, q):
        wait_piece(below, 0, q)
        send_piece(below, 0, q, to_up)
        send_piece(below, 0, q, to_core)
        wait_piece(above, 1, q)
        send_piece(above, 1, q, to_down)
        send_piece(above, 1, q, to_core)

    def rest(below, above, q):
        wait_piece(below, 1, q)
        send_piece(below, 1, q, to_core)
        wait_piece(above, 0, q)
        send_piece(above, 0, q, to_core)

    def from_across(q):
        for h in range(2):
            wait_piece(across, h, q)
        to_z(across, q, True)
        to_z(across, q, False)
        for h in range(2):
            send_piece(across, h, q, to_core)

    def from_far(j, q):
        for h in range(2):
            wait_piece(j, h, q)
            send_piece(j, h, q, to_core)

    for q, (start, size) in enumerate(cuts):
        if q:
            all_slot_copies(q).wait_recv()
        all_slots = slots[q][:, :cap].reshape(MEMBERS * cap, size)
        for h in range(2):
            gath[q][spot_of(d, c, h)] = jnp.dot(
                pick[h * half:(h + 1) * half], all_slots, preferred_element_type=F32
            ).astype(BF16)
        to_z(d, q, True)
        send_piece(d, 0, q, to_across)
        send_piece(d, 1, q, to_across)
        to_z(d, q, False)
        send_piece(d, 0, q, to_core)
        send_piece(d, 1, q, to_core)

    aup, adown, far, afar = chip(True, 1), chip(True, 3), chip(False, 2), chip(True, 2)
    load_g.wait()
    load_u.wait()
    multiply(d, 0, first=True)
    forward(down, up, 0)
    from_across(0)
    rest(down, up, 0)

    relay_counts.wait_recv()
    off = jnp.zeros((1, LANES), F32)
    s_i, r_i = iota((cap, rows), 0), iota((cap, rows), 1)
    for i in range(MEMBERS):
        n = counts_in[i].astype(F32)[0:1]
        hit = (r_i - s_i == off[:, 0:1]) & (s_i < n[:, 0:1])
        place[i * cap:(i + 1) * cap] = jnp.where(hit, 1.0, 0.0).astype(BF16)
        off = off + n

    multiply(d, 1)
    multiply(across, 0)
    forward(down, up, 1)
    multiply(down, 0)
    multiply(up, 0)
    from_across(1)
    relay_x = remote(x_v, x_in, relay_s.at[2], relay_r.at[2], counterpart)
    relay_x.start()
    for q in range(2):
        all_slot_copies(q).wait_send()
    forward(adown, aup, 0)
    rest(adown, aup, 0)
    rest(down, up, 1)
    multiply(across, 1)
    multiply(adown, 0)
    multiply(aup, 0)
    multiply(down, 1)
    multiply(up, 1)
    from_far(far, 0)
    forward(adown, aup, 1)
    from_far(far, 1)
    multiply(far, 0)
    multiply(far, 1)
    rest(adown, aup, 1)
    from_far(afar, 0)
    multiply(adown, 1)
    from_far(afar, 1)
    multiply(afar, 0)
    multiply(aup, 1)
    multiply(afar, 1)

    def activate(n):
        at = pl.ds(pl.multiple_of(n * 128, 128), 128)
        g = acc_g[at]
        hid[at] = (g / (1.0 + jnp.exp(-g)) * acc_u[at]).astype(BF16)

    loop(0, rows // 128, activate)
    pltpu.make_async_copy(wd, wd, load_sem.at[3]).wait()

    order = [(o, s) for o in (True, False) for s in (2, 1, 3, 0)]
    core_copies = {}
    def project(q, k):
        j = chip(*order[k])
        cols = slice(q * LANES, (q + 1) * LANES)
        w = jnp.concatenate([wd[j, 1 - c, :, cols], wd[j, c, :, cols]], axis=1)
        v = jnp.dot(hid[...], w, preferred_element_type=F32)
        core_out[q, k] = v[:, :LANES].astype(BF16)
        cp = remote(
            core_out.at[q, k], core_in.at[q, k], core_s.at[0], core_r.at[q, k], to_core
        )
        cp.start()
        core_copies[q, k] = cp
        own[q, k] = v[:, LANES:]

    def both(q, k, h):
        at = pl.ds(h * half, half)
        return own[q, k, at] + core_in[q, k, at].astype(F32)

    def send_far(q, g):
        core_copies[q, 4 * g].wait_recv()
        for h, device in ((0, to_up), (1, to_down)):
            opp_out[q, g, h] = both(q, 4 * g, h).astype(BF16)
            remote(
                opp_out.at[q, g, h], opp_in.at[q, g, h], opp_s.at[0], opp_r.at[q, g, h], device
            ).start()

    def send_near(q, g, way, h, add):
        v = both(q, 4 * g + 1 + way, h)
        if add:
            v = v + opp_in[q, g, h].astype(F32)
        near_out[q, g, way, h] = v.astype(BF16)
        remote(
            near_out.at[q, g, way, h], near_in.at[q, g, way, h],
            near_s.at[0], near_r.at[q, g], to_down if way else to_up,
        ).start()

    def free_near(q, g):
        for way, h in ((0, 1), (1, 0)):
            core_copies[q, 4 * g + 1 + way].wait_recv()
            send_near(q, g, way, h, False)

    def independent(q):
        for g in range(2):
            send_far(q, g)
        for g in range(2):
            free_near(q, g)

    def dependent_group(q, g):
        for way, h in ((0, 0), (1, 1)):
            remote(
                opp_out.at[q, g, h], opp_in.at[q, g, h],
                opp_s.at[0], opp_r.at[q, g, h], to_up,
            ).wait_recv()
            send_near(q, g, way, h, True)

    def dependent(q):
        for g in range(2):
            dependent_group(q, g)

    def collect_group(q, g):
        core_copies[q, 4 * g + 3].wait_recv()
        remote(
            near_out.at[q, g], near_in.at[q, g], near_s.at[0], near_r.at[q, g], to_up
        ).wait_recv()
        for h in range(2):
            sum_out[q, g, h * half:(h + 1) * half] = (
                both(q, 4 * g + 3, h)
                + near_in[q, g, 0, h].astype(F32)
                + near_in[q, g, 1, h].astype(F32)
            ).astype(BF16)
        remote(
            sum_out.at[q, g], sum_in.at[q, y], sum_s.at[0], sum_r.at[q],
            (after, c, d if g else across),
        ).start()

    def collect(q):
        for g in range(2):
            collect_group(q, g)

    def back_copy(k, q):
        i, device = member(k)
        return remote(
            back_out.at[q, i], back_in.at[q, me], back_s.at[q], back_r.at[q], device
        )

    def all_back_copies(q):
        block = pl.ds(0, MEMBERS - 1)
        return remote(
            back_out.at[q, block], back_in.at[q, block], back_s.at[q], back_r.at[q], to_core
        )

    def unpack(q):
        remote(sum_out.at[q], sum_in.at[q], sum_s.at[0], sum_r.at[q], to_core).wait_recv()
        final = (sum_in[q, 0].astype(F32) + sum_in[q, 1].astype(F32)).astype(BF16)
        back_out[q] = (
            jnp.dot(place[...], final, preferred_element_type=F32)
            .astype(BF16)
            .reshape(MEMBERS, cap, LANES)
        )
        loop(1, MEMBERS, lambda k: back_copy(MEMBERS - k, q).start())
        back_in[q, me] = back_out[q, me]

    def finish(q):
        spread = route_in[:, :cap].astype(BF16)
        scale_in = route_in[:, cap:cap + 1]
        all_back_copies(q).wait_recv()

        for k in range(0, MEMBERS, 2):
            pair = jnp.concatenate([back_in[q, k], back_in[q, k + 1]], axis=1)
            term = scale_in * jnp.dot(spread, pair, preferred_element_type=F32)
            for t in range(2):
                start = (k + t) * part + q * LANES
                at = slice(start, start + LANES)
                v = x_in[:, at].astype(F32) + term[:, t * LANES:(t + 1) * LANES]
                out[:, at] = v.astype(BF16)
                pltpu.make_async_copy(out.at[:, at], out_hbm.at[:, at], out_sem.at[0]).start()

    def projects(q):
        for k in (0, 4, 1, 2, 5, 6, 3, 7):
            project(q, k)

    project(0, 0)
    project(0, 4)
    project(0, 1)
    send_far(0, 0)
    project(0, 2)
    send_far(0, 1)
    project(0, 5)
    project(0, 6)
    free_near(0, 0)
    project(0, 3)
    project(0, 7)
    free_near(0, 1)
    projects(1)
    dependent(0)
    independent(1)
    projects(2)
    collect(0)
    dependent(1)
    send_far(2, 0)
    free_near(2, 0)
    send_far(2, 1)
    collect(1)
    dependent_group(2, 0)
    free_near(2, 1)
    dependent_group(2, 1)
    collect(2)
    unpack(0)
    unpack(1)
    relay_route.wait_recv()
    relay_x.wait_recv()
    unpack(2)
    finish(0)
    finish(1)
    for q in range(2):
        gather_sent(q)
    for src, dst, sem in (
        (core_out, core_in, core_s), (opp_out, opp_in, opp_s),
        (near_out, near_in, near_s), (sum_out, sum_in, sum_s),
    ):
        remote(src, dst, sem.at[0], relay_r.at[0], to_core).wait_send()
    for cp in (relay_route, relay_counts, relay_x):
        cp.wait_send()
    for q in range(strips - 1):
        all_back_copies(q).wait_send()
    finish(2)
    all_back_copies(2).wait_send()
    pltpu.make_async_copy(out, out_hbm, out_sem.at[0]).wait()


def solution(mesh):
    sections = mesh.shape["pipe"]

    def per_device(hidden_in, norm_gain, w_gate, w_up, w_down, expert_ids, gate_weights):
        tokens, width = hidden_in.shape
        ff = w_gate.shape[2]
        cap = tokens // 2
        rows = MEMBERS * cap // 2
        half = rows // 2
        part = width // MEMBERS
        strips = part // LANES
        vmem = pltpu.VMEM
        dma = pltpu.SemaphoreType.DMA
        any_space = pl.BlockSpec(memory_space=pl.ANY)
        return pl.pallas_call(
            functools.partial(kernel, sections),
            out_shape=jax.ShapeDtypeStruct((tokens, width), BF16),
            in_specs=[any_space] * 7,
            out_specs=any_space,
            scratch_shapes=[
                vmem((tokens, width), BF16),
                vmem((tokens, width), BF16),
                vmem((tokens, width), BF16),
                vmem((1, width), F32),
                vmem((2, tokens), jnp.int32),
                vmem((2, tokens), F32),
                vmem((tokens, tokens), F32),
                vmem((tokens, tokens), F32),
                vmem((MEMBERS, TILE, LANES), BF16),
                vmem((MEMBERS, TILE, LANES), BF16),
                vmem((CHIPS, 2, part, ff), BF16),
                vmem((CHIPS, 2, part, ff), BF16),
                vmem((CHIPS, 2, ff, part), BF16),
                vmem((MEMBERS, cap + TILE, LANES), BF16),
                vmem((MEMBERS, cap, part - LANES), BF16),
                vmem((MEMBERS, cap + TILE, LANES), BF16),
                vmem((MEMBERS, cap, part - LANES), BF16),
                vmem((rows, MEMBERS * cap), BF16),
                vmem((MEMBERS * cap, rows), BF16),
                vmem((CHIPS * 4, half, LANES), BF16),
                vmem((CHIPS * 4, half, part - LANES), BF16),
                vmem((rows, ff), F32),
                vmem((rows, ff), F32),
                vmem((rows, ff), BF16),
                vmem((strips, CHIPS, rows, LANES), F32),
                vmem((strips, CHIPS, rows, LANES), BF16),
                vmem((strips, CHIPS, rows, LANES), BF16),
                vmem((strips, 2, 2, half, LANES), BF16),
                vmem((strips, 2, 2, half, LANES), BF16),
                vmem((strips, 2, 2, 2, half, LANES), BF16),
                vmem((strips, 2, 2, 2, half, LANES), BF16),
                vmem((strips, 2, rows, LANES), BF16),
                vmem((strips, 2, rows, LANES), BF16),
                vmem((strips, MEMBERS, cap, LANES), BF16),
                vmem((strips, MEMBERS, cap, LANES), BF16),
                dma((7,)), dma((1,)),
                dma((2,)), dma((2,)),
                dma((2,)), dma((2, CHIPS, 2)), dma((2, CHIPS)),
                dma((1,)), dma((strips, CHIPS)),
                dma((1,)), dma((strips, 2, 2)),
                dma((1,)), dma((strips, 2)),
                dma((1,)), dma((strips,)),
                dma((strips,)), dma((strips,)),
                dma((3,)), dma((3,)),
            ],
            compiler_params=pltpu.CompilerParams(
                collective_id=0, has_side_effects=True, vmem_limit_bytes=62 * 2**20
            ),
            name="routed_block",
        )(
            hidden_in,
            norm_gain,
            w_gate.reshape(CHIPS, 2, part, ff),
            w_up.reshape(CHIPS, 2, part, ff),
            w_down.reshape(ff, width),
            expert_ids.T,
            gate_weights.T,
        )

    return jax.shard_map(
        per_device,
        mesh=mesh,
        in_specs=(
            P(("pipe", "expert", "dp"), None),
            P("pipe", None),
            P("pipe", None, ("expert", "dp")),
            P("pipe", None, ("expert", "dp")),
            P("pipe", ("expert", "dp"), None),
            P(("pipe", "expert", "dp"), None),
            P(("pipe", "expert", "dp"), None),
        ),
        out_specs=P(("pipe", "expert", "dp"), None),
        check_vma=False,
    )
```

```python
import functools

import jax
import jax.numpy as jnp
from jax import lax
from jax.experimental import pallas as pl
from jax.experimental.pallas import tpu as pltpu
from jax.sharding import PartitionSpec as P

MESH = pl.DeviceIdType.MESH
F32 = jnp.float32
BF16 = jnp.bfloat16
CHIPS = 8
MEMBERS = 16
LANES = 128
RELAY_PIECES = 4
TILE = 16


def iota(shape, dim):
    return lax.broadcasted_iota(jnp.int32, shape, dim).astype(F32)


def kernel(
    sections,
    x_hbm, gain_hbm, wg_hbm, wu_hbm, wd_hbm, ids_hbm, gw_hbm,
    out_hbm,
    x_v, x_mid, x_in, out, gain, ids, gw, route, route_in, counts, counts_in, wg, wu, wd,
    packed_0, packed_1, slots_0, slots_1, pick, place, gath_0, gath_1, acc_g, acc_u, hid, own, core_out, core_in, opp_out, opp_in,
    near_out, near_in, sum_out, sum_in, back_out, back_in,
    load_sem, out_sem, a2a_s, a2a_r, gath_s, gath_r, pair_r, core_s, core_r,
    opp_s, opp_r, near_s, near_r, sum_s, sum_r, back_s, back_r, relay_s, relay_r, mid_r,
):
    p, c, d = lax.axis_index("pipe"), lax.axis_index("expert"), lax.axis_index("dp")
    y, z = d // 4, d % 4
    me = d * 2 + c
    after, before = lax.rem(p + 1, sections), lax.rem(p + sections - 1, sections)
    tokens, width = x_v.shape
    packed, slots, gath = (packed_0, packed_1), (slots_0, slots_1), (gath_0, gath_1)
    cap = packed_1.shape[1]
    part = LANES + packed_1.shape[2]
    half = gath_0.shape[1]
    rows = 2 * half
    strips = part // LANES
    cuts = ((0, LANES), (LANES, part - LANES))

    def chip(other_y, step):
        yy = 1 - y if other_y else y
        return yy * 4 + (z + step) % 4

    up, down, across = chip(False, 1), chip(False, 3), chip(True, 0)
    to_up, to_down, to_across = (p, c, up), (p, c, down), (p, c, across)
    to_core = (p, 1 - c, d)

    def remote(src, dst, send, recv, device):
        return pltpu.make_async_remote_copy(
            src_ref=src, dst_ref=dst, send_sem=send, recv_sem=recv,
            device_id=device, device_id_type=MESH,
        )

    def loop(first, last, body):
        def step(k, carry):
            body(k)
            return carry

        lax.fori_loop(first, last, step, 0)

    def member(k):
        dd = (y + k // 8) % 2 * 4 + (z + k // 2) % 4
        e = (c + k) % 2
        return dd * 2 + e, (p, e, dd)

    load_x = pltpu.make_async_copy(x_hbm, x_v, load_sem.at[0])
    load_g = pltpu.make_async_copy(wg_hbm, wg, load_sem.at[1])
    load_u = pltpu.make_async_copy(wu_hbm, wu, load_sem.at[2])
    small = [
        pltpu.make_async_copy(src, dst, load_sem.at[4 + n])
        for n, (src, dst) in enumerate(((ids_hbm, ids), (gw_hbm, gw), (gain_hbm, gain)))
    ]
    small[0].start()
    small[1].start()
    load_x.start()
    small[2].start()

    barrier = pltpu.get_barrier_semaphore()

    def greet(device):
        pl.semaphore_signal(barrier, inc=1, device_id=device, device_id_type=MESH)

    loop(1, MEMBERS, lambda k: greet(member(k)[1]))
    greet((before, c, d))
    greet((before, c, across))

    small[0].wait()
    small[1].wait()
    square = (tokens, tokens)
    chosen = ids[...] == 0
    routed = jnp.max(jnp.where(chosen, 1.0, 0.0), axis=0, keepdims=True)
    weight = jnp.sum(jnp.where(chosen, gw[...], 0.0), axis=0, keepdims=True)
    routed_b = jnp.broadcast_to(routed, square)
    tri = jnp.where(iota(square, 0) <= iota(square, 1), 1.0, 0.0).astype(BF16)
    rank = jnp.dot(routed_b.astype(BF16), tri, preferred_element_type=F32)
    spot = jnp.where((routed_b > 0.5) & (rank - 1.0 == iota(square, 0)), 1.0, 0.0)
    spot_t = spot[:cap].astype(BF16)
    route[...] = jnp.where(
        iota(square, 1) < cap, spot.T, jnp.broadcast_to(weight, square).T
    )
    count = jnp.dot(
        routed_b[:TILE].astype(BF16), jnp.ones(square, BF16), preferred_element_type=F32
    ).astype(BF16)
    for i in range(MEMBERS):
        packed_0[i, cap:] = count

    load_x.wait()
    small[2].wait()
    load_g.start()
    load_u.start()
    for j in range(CHIPS):
        for e in range(2):
            pltpu.make_async_copy(
                wd_hbm.at[:, pl.ds((2 * j + e) * part, part)], wd.at[j, e], load_sem.at[3]
            ).start()

    def squares(j, total):
        for t in range(strips):
            at = pl.ds(pl.multiple_of(j * part + t * LANES, LANES), LANES)
            v = x_v[:, at].astype(F32)
            total = total + v * v
        return total

    total = lax.fori_loop(0, MEMBERS, squares, jnp.zeros((tokens, LANES), F32))
    scale = lax.rsqrt(jnp.sum(total, axis=1, keepdims=True) / width + 1e-05)

    def pack(j, q):
        start, size = cuts[q]
        for t in range(4):
            i = j * 4 + t
            at = pl.ds(pl.multiple_of(i * part + start, LANES), size)
            n = (x_v[:, at].astype(F32) * scale * gain[:, at]).astype(BF16)
            packed[q][i, :cap] = jnp.dot(
                spot_t, n, preferred_element_type=F32
            ).astype(BF16)

    loop(0, MEMBERS // 4, lambda j: pack(j, 0))
    pl.semaphore_wait(barrier, MEMBERS + 1)

    def slot_copy(k, q):
        i, device = member(k)
        return remote(
            packed[q].at[i], slots[q].at[me], a2a_s.at[q], a2a_r.at[q], device
        )

    def all_slot_copies(q):
        block = pl.ds(0, MEMBERS - 1)
        return remote(
            packed[q].at[block], slots[q].at[block], a2a_s.at[q], a2a_r.at[q], to_core
        )

    loop(1, MEMBERS, lambda k: slot_copy(MEMBERS - k, 0).start())
    loop(0, MEMBERS // 4, lambda j: pack(j, 1))
    loop(1, MEMBERS, lambda k: slot_copy(MEMBERS - k, 1).start())

    def relay_piece(i):
        at = pl.ds(i * (tokens // RELAY_PIECES), tokens // RELAY_PIECES)
        return remote(
            x_v.at[at], x_mid.at[at], relay_s.at[2], mid_r.at[i], (after, c, across)
        )

    def relay_on(i):
        relay_piece(i).wait_recv()
        at = pl.ds(i * (tokens // RELAY_PIECES), tokens // RELAY_PIECES)
        remote(x_mid.at[at], x_in.at[at], relay_s.at[3], relay_r.at[2], to_across).start()

    for i in range(RELAY_PIECES):
        relay_piece(i).start()
    for q in range(2):
        slots[q][me] = packed[q][me]
    all_slot_copies(0).wait_recv()
    counts[...] = slots_0[:, cap:]
    counterpart = (after, c, d)
    relay_route = remote(route, route_in, relay_s.at[0], relay_r.at[0], counterpart)
    relay_route.start()
    relay_counts = remote(counts, counts_in, relay_s.at[1], relay_r.at[1], counterpart)
    relay_counts.start()

    off = jnp.zeros((1, LANES), F32)
    lane1 = iota((1, LANES), 1)
    high = lane1 - cap
    row_i = iota((rows, LANES), 0)
    for q in range(MEMBERS // 2):
        n0, n1 = counts[2 * q].astype(F32)[0:1], counts[2 * q + 1].astype(F32)[0:1]
        target = jnp.where(
            lane1 < cap,
            jnp.where(lane1 < n0, off + lane1, -1.0),
            jnp.where(high < n1, off + n0 + high, -1.0),
        )
        pick[:, q * LANES:(q + 1) * LANES] = jnp.where(row_i == target, 1.0, 0.0).astype(BF16)
        off = off + n0 + n1

    sends = [0, 0]

    def spot_of(j, e, h):
        return (j * 2 + e) * 2 + h

    def send_piece(j, h, q, *devices):
        ref = gath[q].at[spot_of(j, c, h)]
        for device in devices:
            sem = (pair_r if device is to_core else gath_r).at[q, j, h]
            remote(ref, ref, gath_s.at[q], sem, device).start()
            sends[q] += 1

    def take_piece(j, h, q, *devices):
        ref = gath[q].at[spot_of(j, c, h)]
        remote(ref, ref, gath_s.at[q], gath_r.at[q, j, h], to_core).wait_recv()
        send_piece(j, h, q, *devices, to_core)

    def gather_sent(q):
        ref = gath[q].at[pl.ds(0, sends[q])]
        remote(ref, ref, gath_s.at[q], gath_r.at[q, 0, 0], to_core).wait_send()

    def multiply(j, q, h, first=False):
        other = gath[q].at[spot_of(j, 1 - c, h)]
        remote(other, other, gath_s.at[q], pair_r.at[q, j, h], to_core).wait_recv()
        start, size = cuts[q]
        cols = slice(start, start + size)
        at = slice(h * half, (h + 1) * half)
        a = jnp.concatenate([gath[q][spot_of(j, e, h)] for e in range(2)], axis=1)
        for w, acc in ((wg, acc_g), (wu, acc_u)):
            b = jnp.concatenate([w[j, e, cols] for e in range(2)], axis=0)
            v = jnp.dot(a, b, preferred_element_type=F32)
            if first:
                acc[at] = v
            else:
                acc[at] += v

    for q, (start, size) in enumerate(cuts):
        if q:
            all_slot_copies(q).wait_recv()
        all_slots = slots[q][:, :cap].reshape(MEMBERS * cap, size)
        for h in range(2):
            gath[q][spot_of(d, c, h)] = jnp.dot(
                pick[h * half:(h + 1) * half], all_slots, preferred_element_type=F32
            ).astype(BF16)
            if h == 0 or q == 0:
                send_piece(d, h, q, to_up)
            send_piece(d, h, q, to_down, to_across, to_core)

    aup, adown, far, afar = chip(True, 1), chip(True, 3), chip(False, 2), chip(True, 2)
    load_g.wait()
    load_u.wait()
    multiply(d, 0, 0, first=True)
    multiply(d, 0, 1, first=True)
    take_piece(down, 0, 0, to_up)
    take_piece(up, 1, 0, to_down)
    take_piece(up, 0, 0)
    take_piece(down, 1, 0)
    multiply(d, 1, 0)
    multiply(d, 1, 1)
    take_piece(across, 0, 0, to_up, to_down)
    take_piece(across, 1, 0, to_down)
    multiply(down, 0, 0)
    multiply(up, 0, 0)
    take_piece(across, 0, 1, to_up, to_down)
    take_piece(down, 0, 1, to_up)
    take_piece(up, 0, 1)
    multiply(across, 0, 0)
    multiply(across, 0, 1)
    multiply(down, 0, 1)
    multiply(up, 0, 1)
    take_piece(across, 1, 1, to_down)
    relay_on(0)
    relay_on(1)
    for q in range(2):
        all_slot_copies(q).wait_send()
    take_piece(adown, 0, 0, to_up)
    take_piece(up, 1, 1, to_down)
    take_piece(far, 0, 0)
    multiply(across, 1, 0)
    multiply(down, 1, 0)
    multiply(up, 1, 0)
    multiply(far, 0, 0)

    take_piece(aup, 0, 0)
    take_piece(adown, 0, 1, to_up)
    send_piece(d, 1, 1, to_up)
    send_piece(across, 1, 0, to_up)
    send_piece(across, 1, 1, to_up)
    multiply(up, 1, 1)
    take_piece(aup, 1, 0, to_down)
    take_piece(far, 1, 0)
    multiply(across, 1, 1)
    multiply(adown, 0, 0)
    multiply(aup, 0, 0)
    multiply(adown, 1, 0)
    multiply(far, 0, 1)
    multiply(aup, 0, 1)
    take_piece(far, 0, 1)
    take_piece(aup, 0, 1)
    take_piece(afar, 0, 0)
    multiply(far, 1, 0)
    multiply(aup, 1, 0)
    take_piece(aup, 1, 1, to_down)
    relay_on(2)
    multiply(afar, 0, 0)
    take_piece(afar, 0, 1)
    multiply(aup, 1, 1)
    multiply(afar, 1, 0)

    def activate(h):
        def block(n):
            at = pl.ds(pl.multiple_of(h * half + n * 128, 128), 128)
            g = acc_g[at]
            hid[at] = (g / (1.0 + jnp.exp(-g)) * acc_u[at]).astype(BF16)

        loop(0, half // 128, block)

    FAR, UP, DOWN, HERE = range(4)
    steps = (2, 1, 3, 0)

    def core_copy(q, h, t):
        return remote(
            core_out.at[q, h, t], core_in.at[q, h, t], core_s.at[0], core_r.at[q, h, t], to_core
        )

    def project(q, h, *targets):
        cols = slice(q * LANES, (q + 1) * LANES)
        for t in targets:
            chips = (chip(True, steps[t]), chip(False, steps[t]))
            w = jnp.concatenate(
                [wd[j, e, :, cols] for j in chips for e in (1 - c, c)], axis=1
            )
            v = jnp.dot(hid[h * half:(h + 1) * half], w, preferred_element_type=F32)
            for g in range(2):
                core_out[q, h, t, g] = v[:, 2 * g * LANES:(2 * g + 1) * LANES].astype(BF16)
                own[q, h, t, g] = v[:, (2 * g + 1) * LANES:(2 * g + 2) * LANES]
            core_copy(q, h, t).start()

    def both(q, h, t):
        return own[q, h, t] + core_in[q, h, t].astype(F32)

    def far_copy(q, h):
        return remote(
            opp_out.at[q, h], opp_in.at[q, h], opp_s.at[0], opp_r.at[q, h],
            to_down if h else to_up,
        )

    def send_far(q, h):
        core_copy(q, h, FAR).wait_recv()
        opp_out[q, h] = both(q, h, FAR).astype(BF16)
        far_copy(q, h).start()

    def send_near(q, h, way, v):
        near_out[q, h, way] = v.astype(BF16)
        remote(
            near_out.at[q, h, way], near_in.at[q, h, way], near_s.at[0], near_r.at[q, h],
            to_down if way else to_up,
        ).start()

    def send_free(q, h):
        t = UP if h else DOWN
        core_copy(q, h, t).wait_recv()
        send_near(q, h, 1 - h, both(q, h, t))

    def send_joined(q, h):
        t = DOWN if h else UP
        core_copy(q, h, t).wait_recv()
        far_copy(q, h).wait_recv()
        send_near(q, h, h, both(q, h, t) + opp_in[q, h].astype(F32))

    def collect(q, h):
        core_copy(q, h, HERE).wait_recv()
        remote(
            near_out.at[q, h], near_in.at[q, h], near_s.at[0], near_r.at[q, h], to_up
        ).wait_recv()
        sum_out[q, h] = (
            both(q, h, HERE) + near_in[q, h, 0].astype(F32) + near_in[q, h, 1].astype(F32)
        ).astype(BF16)
        for g in range(2):
            remote(
                sum_out.at[q, h, g], sum_in.at[q, y, h], sum_s.at[0], sum_r.at[q],
                (after, c, d if g else across),
            ).start()

    def back_copy(k, q):
        i, device = member(k)
        return remote(
            back_out.at[q, i], back_in.at[q, me], back_s.at[q], back_r.at[q], device
        )

    def all_back_copies(q):
        block = pl.ds(0, MEMBERS - 1)
        return remote(
            back_out.at[q, block], back_in.at[q, block], back_s.at[q], back_r.at[q], to_core
        )

    def unpack(q):
        remote(sum_out.at[q], sum_in.at[q], sum_s.at[0], sum_r.at[q], to_core).wait_recv()
        final = (sum_in[q, 0].astype(F32) + sum_in[q, 1].astype(F32)).astype(BF16)
        final = final.reshape(rows, LANES)
        back_out[q] = (
            jnp.dot(place[...], final, preferred_element_type=F32)
            .astype(BF16)
            .reshape(MEMBERS, cap, LANES)
        )
        loop(1, MEMBERS, lambda k: back_copy(MEMBERS - k, q).start())
        back_in[q, me] = back_out[q, me]

    def finish(q):
        spread = route_in[:, :cap].astype(BF16)
        scale_in = route_in[:, cap:cap + 1]
        all_back_copies(q).wait_recv()

        for k in range(0, MEMBERS, 2):
            pair = jnp.concatenate([back_in[q, k], back_in[q, k + 1]], axis=1)
            term = scale_in * jnp.dot(spread, pair, preferred_element_type=F32)
            for t in range(2):
                start = (k + t) * part + q * LANES
                at = slice(start, start + LANES)
                v = x_in[:, at].astype(F32) + term[:, t * LANES:(t + 1) * LANES]
                out[:, at] = v.astype(BF16)
                pltpu.make_async_copy(out.at[:, at], out_hbm.at[:, at], out_sem.at[0]).start()

    activate(0)
    pltpu.make_async_copy(wd, wd, load_sem.at[3]).wait()
    project(0, 0, FAR, DOWN, UP)
    take_piece(far, 1, 1)
    take_piece(down, 1, 1)
    send_far(0, 0)
    send_free(0, 0)
    project(0, 0, HERE)
    project(1, 0, FAR, DOWN, UP)
    take_piece(afar, 1, 0)
    take_piece(adown, 1, 0)
    multiply(far, 1, 1)
    send_far(1, 0)
    send_free(1, 0)
    multiply(down, 1, 1)
    multiply(afar, 0, 1)
    multiply(adown, 0, 1)
    project(1, 0, HERE)
    project(2, 0, FAR, DOWN, UP)
    relay_on(3)
    take_piece(afar, 1, 1)
    take_piece(adown, 1, 1)
    send_far(2, 0)
    send_free(2, 0)
    project(2, 0, HERE)
    multiply(afar, 1, 1)
    multiply(adown, 1, 1)
    activate(1)
    send_joined(0, 0)
    project(0, 1, FAR, UP, DOWN)
    send_far(0, 1)
    project(0, 1, HERE)
    project(1, 1, FAR)
    send_joined(1, 0)
    send_free(0, 1)
    project(1, 1, UP, DOWN)
    send_far(1, 1)
    project(1, 1, HERE)
    project(2, 1, FAR)
    send_joined(2, 0)
    send_free(1, 1)
    project(2, 1, UP, DOWN)
    send_far(2, 1)
    send_free(2, 1)
    project(2, 1, HERE)

    relay_counts.wait_recv()
    off = jnp.zeros((1, LANES), F32)
    s_i, r_i = iota((cap, rows), 0), iota((cap, rows), 1)
    for i in range(MEMBERS):
        n = counts_in[i].astype(F32)[0:1]
        hit = (r_i - s_i == off[:, 0:1]) & (s_i < n[:, 0:1])
        place[i * cap:(i + 1) * cap] = jnp.where(hit, 1.0, 0.0).astype(BF16)
        off = off + n

    collect(0, 0)
    send_joined(0, 1)
    collect(1, 0)
    send_joined(1, 1)
    send_joined(2, 1)
    collect(2, 0)
    collect(0, 1)
    collect(1, 1)
    collect(2, 1)
    unpack(0)
    unpack(1)
    relay_route.wait_recv()
    relay_x = remote(x_mid, x_in, relay_s.at[3], relay_r.at[2], to_across)
    relay_x.wait_recv()
    unpack(2)
    finish(0)
    finish(1)
    for q in range(2):
        gather_sent(q)
    for src, dst, sem in (
        (core_out, core_in, core_s), (opp_out, opp_in, opp_s),
        (near_out, near_in, near_s), (sum_out, sum_in, sum_s),
    ):
        remote(src, dst, sem.at[0], relay_r.at[0], to_core).wait_send()
    relay_first = remote(x_v, x_mid, relay_s.at[2], mid_r.at[0], to_across)
    for cp in (relay_route, relay_counts, relay_first, relay_x):
        cp.wait_send()
    for q in range(strips - 1):
        all_back_copies(q).wait_send()
    finish(2)
    all_back_copies(2).wait_send()
    pltpu.make_async_copy(out, out_hbm, out_sem.at[0]).wait()


def solution(mesh):
    sections = mesh.shape["pipe"]

    def per_device(hidden_in, norm_gain, w_gate, w_up, w_down, expert_ids, gate_weights):
        tokens, width = hidden_in.shape
        ff = w_gate.shape[2]
        cap = tokens // 2
        rows = MEMBERS * cap // 2
        half = rows // 2
        part = width // MEMBERS
        strips = part // LANES
        vmem = pltpu.VMEM
        dma = pltpu.SemaphoreType.DMA
        any_space = pl.BlockSpec(memory_space=pl.ANY)
        return pl.pallas_call(
            functools.partial(kernel, sections),
            out_shape=jax.ShapeDtypeStruct((tokens, width), BF16),
            in_specs=[any_space] * 7,
            out_specs=any_space,
            scratch_shapes=[
                vmem((tokens, width), BF16),
                vmem((tokens, width), BF16),
                vmem((tokens, width), BF16),
                vmem((tokens, width), BF16),
                vmem((1, width), F32),
                vmem((2, tokens), jnp.int32),
                vmem((2, tokens), F32),
                vmem((tokens, tokens), F32),
                vmem((tokens, tokens), F32),
                vmem((MEMBERS, TILE, LANES), BF16),
                vmem((MEMBERS, TILE, LANES), BF16),
                vmem((CHIPS, 2, part, ff), BF16),
                vmem((CHIPS, 2, part, ff), BF16),
                vmem((CHIPS, 2, ff, part), BF16),
                vmem((MEMBERS, cap + TILE, LANES), BF16),
                vmem((MEMBERS, cap, part - LANES), BF16),
                vmem((MEMBERS, cap + TILE, LANES), BF16),
                vmem((MEMBERS, cap, part - LANES), BF16),
                vmem((rows, MEMBERS * cap), BF16),
                vmem((MEMBERS * cap, rows), BF16),
                vmem((CHIPS * 4, half, LANES), BF16),
                vmem((CHIPS * 4, half, part - LANES), BF16),
                vmem((rows, ff), F32),
                vmem((rows, ff), F32),
                vmem((rows, ff), BF16),
                vmem((strips, 2, 4, 2, half, LANES), F32),
                vmem((strips, 2, 4, 2, half, LANES), BF16),
                vmem((strips, 2, 4, 2, half, LANES), BF16),
                vmem((strips, 2, 2, half, LANES), BF16),
                vmem((strips, 2, 2, half, LANES), BF16),
                vmem((strips, 2, 2, 2, half, LANES), BF16),
                vmem((strips, 2, 2, 2, half, LANES), BF16),
                vmem((strips, 2, 2, half, LANES), BF16),
                vmem((strips, 2, 2, half, LANES), BF16),
                vmem((strips, MEMBERS, cap, LANES), BF16),
                vmem((strips, MEMBERS, cap, LANES), BF16),
                dma((7,)), dma((1,)),
                dma((2,)), dma((2,)),
                dma((2,)), dma((2, CHIPS, 2)), dma((2, CHIPS, 2)),
                dma((1,)), dma((strips, 2, 4)),
                dma((1,)), dma((strips, 2)),
                dma((1,)), dma((strips, 2)),
                dma((1,)), dma((strips,)),
                dma((strips,)), dma((strips,)),
                dma((4,)), dma((3,)), dma((RELAY_PIECES,)),
            ],
            compiler_params=pltpu.CompilerParams(
                collective_id=0, has_side_effects=True, vmem_limit_bytes=62 * 2**20
            ),
            name="routed_block",
        )(
            hidden_in,
            norm_gain,
            w_gate.reshape(CHIPS, 2, part, ff),
            w_up.reshape(CHIPS, 2, part, ff),
            w_down.reshape(ff, width),
            expert_ids.T,
            gate_weights.T,
        )

    return jax.shard_map(
        per_device,
        mesh=mesh,
        in_specs=(
            P(("pipe", "expert", "dp"), None),
            P("pipe", None),
            P("pipe", None, ("expert", "dp")),
            P("pipe", None, ("expert", "dp")),
            P("pipe", ("expert", "dp"), None),
            P(("pipe", "expert", "dp"), None),
            P(("pipe", "expert", "dp"), None),
        ),
        out_specs=P(("pipe", "expert", "dp"), None),
        check_vma=False,
    )
```

```python
import functools

import jax
import jax.numpy as jnp
from jax import lax
from jax.experimental import pallas as pl
from jax.experimental.pallas import tpu as pltpu
from jax.sharding import PartitionSpec as P

MESH = pl.DeviceIdType.MESH
F32 = jnp.float32
BF16 = jnp.bfloat16
CHIPS = 8
MEMBERS = 16
LANES = 128
RELAY_PIECES = 4
X_LOADS = 4
FINISH_STEPS = 4
TILE = 16


def iota(shape, dim):
    return lax.broadcasted_iota(jnp.int32, shape, dim).astype(F32)


def kernel(
    sections,
    x_hbm, gain_hbm, wg_hbm, wu_hbm, wd_hbm, ids_hbm, gw_hbm,
    x_in, back_in, route_in,
    x_v, x_mid, gain, ids, gw, route, counts, counts_in, wg, wu, wd,
    packed_0, packed_1, slots_0, slots_1, pick, place, gath_0, gath_1, acc_g, acc_u, hid, own, core_out, core_in, opp_out, opp_in,
    near_out, near_in, sum_out, sum_in, partial, back_out,
    load_sem, out_sem, a2a_s, a2a_r, gath_s, gath_r, pair_r, core_s, core_r,
    opp_s, opp_r, near_s, near_r, sum_s, sum_r, back_s, back_r, relay_s, relay_r, mid_r,
):
    p, c, d = lax.axis_index("pipe"), lax.axis_index("expert"), lax.axis_index("dp")
    y, z = d // 4, d % 4
    me = d * 2 + c
    after, before = lax.rem(p + 1, sections), lax.rem(p + sections - 1, sections)
    tokens, width = x_v.shape
    packed, slots, gath = (packed_0, packed_1), (slots_0, slots_1), (gath_0, gath_1)
    cap = packed_1.shape[1]
    part = LANES + packed_1.shape[2]
    half = gath_0.shape[1]
    rows = 2 * half
    strips = part // LANES
    cuts = ((0, LANES), (LANES, part - LANES))

    def chip(other_y, step):
        yy = 1 - y if other_y else y
        return yy * 4 + (z + step) % 4

    up, down, across = chip(False, 1), chip(False, 3), chip(True, 0)
    to_up, to_down, to_across = (p, c, up), (p, c, down), (p, c, across)
    to_core = (p, 1 - c, d)

    def remote(src, dst, send, recv, device):
        return pltpu.make_async_remote_copy(
            src_ref=src, dst_ref=dst, send_sem=send, recv_sem=recv,
            device_id=device, device_id_type=MESH,
        )

    def loop(first, last, body):
        def step(k, carry):
            body(k)
            return carry

        lax.fori_loop(first, last, step, 0)

    def member(k):
        dd = (y + k // 8) % 2 * 4 + (z + k // 2) % 4
        e = (c + k) % 2
        return dd * 2 + e, (p, e, dd)

    block = width // X_LOADS
    loads_x = [
        pltpu.make_async_copy(
            x_hbm.at[:, pl.ds(n * block, block)], x_v.at[:, pl.ds(n * block, block)],
            load_sem.at[6 + n],
        )
        for n in range(X_LOADS)
    ]
    load_g = pltpu.make_async_copy(wg_hbm, wg, load_sem.at[0])
    load_u = pltpu.make_async_copy(wu_hbm, wu, load_sem.at[1])
    small = [
        pltpu.make_async_copy(src, dst, load_sem.at[3 + n])
        for n, (src, dst) in enumerate(((ids_hbm, ids), (gw_hbm, gw), (gain_hbm, gain)))
    ]
    small[0].start()
    small[1].start()
    for cp in loads_x:
        cp.start()
    small[2].start()

    barrier = pltpu.get_barrier_semaphore()

    def greet(device):
        pl.semaphore_signal(barrier, inc=1, device_id=device, device_id_type=MESH)

    loop(1, MEMBERS, lambda k: greet(member(k)[1]))
    greet((before, c, d))
    greet((before, c, across))

    small[0].wait()
    small[1].wait()
    square = (tokens, tokens)
    chosen = ids[...] == 0
    routed = jnp.max(jnp.where(chosen, 1.0, 0.0), axis=0, keepdims=True)
    weight = jnp.sum(jnp.where(chosen, gw[...], 0.0), axis=0, keepdims=True)
    routed_b = jnp.broadcast_to(routed, square)
    tri = jnp.where(iota(square, 0) <= iota(square, 1), 1.0, 0.0).astype(BF16)
    rank = jnp.dot(routed_b.astype(BF16), tri, preferred_element_type=F32)
    spot = jnp.where((routed_b > 0.5) & (rank - 1.0 == iota(square, 0)), 1.0, 0.0)
    spot_t = spot[:cap].astype(BF16)
    route[...] = jnp.where(
        iota(square, 1) < cap, spot.T, jnp.broadcast_to(weight, square).T
    )
    count = jnp.dot(
        routed_b[:TILE].astype(BF16), jnp.ones(square, BF16), preferred_element_type=F32
    ).astype(BF16)
    for i in range(MEMBERS):
        packed_0[i, cap:] = count

    total = jnp.zeros((tokens, LANES), F32)
    for n, cp in enumerate(loads_x):
        cp.wait()
        for t in range(block // LANES):
            start = n * block + t * LANES
            v = x_v[:, start:start + LANES].astype(F32)
            total = total + v * v
    scale = lax.rsqrt(jnp.sum(total, axis=1, keepdims=True) / width + 1e-05)
    small[2].wait()
    load_g.start()
    load_u.start()
    for j in range(CHIPS):
        for e in range(2):
            pltpu.make_async_copy(
                wd_hbm.at[:, pl.ds((2 * j + e) * part, part)], wd.at[j, e], load_sem.at[2]
            ).start()

    def pack(j, q):
        start, size = cuts[q]
        for t in range(4):
            i = j * 4 + t
            at = pl.ds(pl.multiple_of(i * part + start, LANES), size)
            n = (x_v[:, at].astype(F32) * scale * gain[:, at]).astype(BF16)
            packed[q][i, :cap] = jnp.dot(
                spot_t, n, preferred_element_type=F32
            ).astype(BF16)

    loop(0, MEMBERS // 4, lambda j: pack(j, 0))
    pl.semaphore_wait(barrier, MEMBERS + 1)

    def slot_copy(k, q):
        i, device = member(k)
        return remote(
            packed[q].at[i], slots[q].at[me], a2a_s.at[q], a2a_r.at[q], device
        )

    def all_slot_copies(q):
        block = pl.ds(0, MEMBERS - 1)
        return remote(
            packed[q].at[block], slots[q].at[block], a2a_s.at[q], a2a_r.at[q], to_core
        )

    for k in range(MEMBERS - 1, 0, -1):
        slot_copy(k, 0).start()
    loop(0, MEMBERS // 4, lambda j: pack(j, 1))
    for k in range(MEMBERS - 1, 0, -1):
        slot_copy(k, 1).start()

    def relay_piece(i):
        at = pl.ds(i * (tokens // RELAY_PIECES), tokens // RELAY_PIECES)
        return remote(
            x_v.at[at], x_mid.at[at], relay_s.at[2], mid_r.at[i], (after, c, across)
        )

    def relay_on(i):
        relay_piece(i).wait_recv()
        at = pl.ds(i * (tokens // RELAY_PIECES), tokens // RELAY_PIECES)
        remote(x_mid.at[at], x_in.at[at], relay_s.at[3], relay_r.at[2], to_across).start()

    for i in range(RELAY_PIECES):
        relay_piece(i).start()
    for q in range(2):
        slots[q][me] = packed[q][me]
    all_slot_copies(0).wait_recv()
    counts[...] = slots_0[:, cap:]
    counterpart = (after, c, d)
    relay_route = remote(route, route_in, relay_s.at[0], relay_r.at[0], counterpart)
    relay_route.start()
    relay_counts = remote(counts, counts_in, relay_s.at[1], relay_r.at[1], counterpart)
    relay_counts.start()

    off = jnp.zeros((1, LANES), F32)
    lane1 = iota((1, LANES), 1)
    high = lane1 - cap
    row_i = iota((rows, LANES), 0)
    for q in range(MEMBERS // 2):
        n0, n1 = counts[2 * q].astype(F32)[0:1], counts[2 * q + 1].astype(F32)[0:1]
        target = jnp.where(
            lane1 < cap,
            jnp.where(lane1 < n0, off + lane1, -1.0),
            jnp.where(high < n1, off + n0 + high, -1.0),
        )
        pick[:, q * LANES:(q + 1) * LANES] = jnp.where(row_i == target, 1.0, 0.0).astype(BF16)
        off = off + n0 + n1

    sends = [0, 0]

    def spot_of(j, e, h):
        return (j * 2 + e) * 2 + h

    def send_piece(j, h, q, *devices):
        ref = gath[q].at[spot_of(j, c, h)]
        for device in devices:
            sem = (pair_r if device is to_core else gath_r).at[q, j, h]
            remote(ref, ref, gath_s.at[q], sem, device).start()
            sends[q] += 1

    def take_piece(j, h, q, *devices):
        ref = gath[q].at[spot_of(j, c, h)]
        remote(ref, ref, gath_s.at[q], gath_r.at[q, j, h], to_core).wait_recv()
        send_piece(j, h, q, *devices, to_core)

    def gather_sent(q):
        ref = gath[q].at[pl.ds(0, sends[q])]
        remote(ref, ref, gath_s.at[q], gath_r.at[q, 0, 0], to_core).wait_send()

    def multiply(j, q, h, first=False):
        other = gath[q].at[spot_of(j, 1 - c, h)]
        remote(other, other, gath_s.at[q], pair_r.at[q, j, h], to_core).wait_recv()
        start, size = cuts[q]
        cols = slice(start, start + size)
        at = slice(h * half, (h + 1) * half)
        a = jnp.concatenate([gath[q][spot_of(j, e, h)] for e in range(2)], axis=1)
        for w, acc in ((wg, acc_g), (wu, acc_u)):
            b = jnp.concatenate([w[j, e, cols] for e in range(2)], axis=0)
            v = jnp.dot(a, b, preferred_element_type=F32)
            if first:
                acc[at] = v
            else:
                acc[at] += v

    for q, (start, size) in enumerate(cuts):
        if q:
            all_slot_copies(q).wait_recv()
        all_slots = slots[q][:, :cap].reshape(MEMBERS * cap, size)
        for h in range(2):
            gath[q][spot_of(d, c, h)] = jnp.dot(
                pick[h * half:(h + 1) * half], all_slots, preferred_element_type=F32
            ).astype(BF16)
            if h == 0 or q == 0:
                send_piece(d, h, q, to_up)
            send_piece(d, h, q, to_down, to_across, to_core)

    aup, adown, far, afar = chip(True, 1), chip(True, 3), chip(False, 2), chip(True, 2)
    load_g.wait()
    load_u.wait()
    multiply(d, 0, 0, first=True)
    multiply(d, 0, 1, first=True)
    take_piece(down, 0, 0, to_up)
    take_piece(up, 1, 0, to_down)
    take_piece(up, 0, 0)
    take_piece(down, 1, 0)
    multiply(d, 1, 0)
    multiply(d, 1, 1)
    take_piece(across, 0, 0, to_up, to_down)
    take_piece(across, 1, 0, to_down)
    multiply(down, 0, 0)
    multiply(up, 0, 0)
    take_piece(across, 0, 1, to_up, to_down)
    take_piece(down, 0, 1, to_up)
    take_piece(up, 0, 1)
    multiply(across, 0, 0)
    multiply(across, 0, 1)
    multiply(down, 0, 1)
    multiply(up, 0, 1)
    take_piece(across, 1, 1, to_down)
    relay_on(0)
    for q in range(2):
        all_slot_copies(q).wait_send()
    take_piece(adown, 0, 0, to_up)
    take_piece(up, 1, 1, to_down)
    take_piece(far, 0, 0)
    multiply(across, 1, 0)
    multiply(down, 1, 0)
    multiply(up, 1, 0)
    multiply(far, 0, 0)

    relay_on(1)
    take_piece(aup, 0, 0)
    take_piece(adown, 0, 1, to_up)
    send_piece(d, 1, 1, to_up)
    send_piece(across, 1, 0, to_up)
    send_piece(across, 1, 1, to_up)
    multiply(up, 1, 1)
    take_piece(aup, 1, 0, to_down)
    take_piece(far, 1, 0)
    multiply(across, 1, 1)
    multiply(adown, 0, 0)
    multiply(aup, 0, 0)
    multiply(adown, 1, 0)
    multiply(far, 0, 1)
    multiply(aup, 0, 1)
    take_piece(far, 0, 1)
    take_piece(aup, 0, 1)
    take_piece(afar, 0, 0)
    multiply(far, 1, 0)
    multiply(aup, 1, 0)
    take_piece(aup, 1, 1, to_down)
    relay_on(2)
    multiply(afar, 0, 0)
    take_piece(afar, 0, 1)
    multiply(aup, 1, 1)
    multiply(afar, 1, 0)

    def activate(h):
        def block(n):
            at = pl.ds(pl.multiple_of(h * half + n * 128, 128), 128)
            g = acc_g[at]
            hid[at] = (g / (1.0 + jnp.exp(-g)) * acc_u[at]).astype(BF16)

        loop(0, half // 128, block)

    FAR, UP, DOWN, HERE = range(4)
    steps = (2, 1, 3, 0)

    def core_copy(q, h, t):
        return remote(
            core_out.at[q, h, t], core_in.at[q, h, t], core_s.at[0], core_r.at[q, h, t], to_core
        )

    def project(q, h, *targets):
        cols = slice(q * LANES, (q + 1) * LANES)
        for t in targets:
            chips = (chip(True, steps[t]), chip(False, steps[t]))
            w = jnp.concatenate(
                [wd[j, e, :, cols] for j in chips for e in (1 - c, c)], axis=1
            )
            v = jnp.dot(hid[h * half:(h + 1) * half], w, preferred_element_type=F32)
            for g in range(2):
                core_out[q, h, t, g] = v[:, 2 * g * LANES:(2 * g + 1) * LANES].astype(BF16)
                own[q, h, t, g] = v[:, (2 * g + 1) * LANES:(2 * g + 2) * LANES]
            core_copy(q, h, t).start()

    def both(q, h, t):
        return own[q, h, t] + core_in[q, h, t].astype(F32)

    def far_copy(q, h):
        return remote(
            opp_out.at[q, h], opp_in.at[q, h], opp_s.at[0], opp_r.at[q, h],
            to_down if h else to_up,
        )

    def send_far(q, h):
        core_copy(q, h, FAR).wait_recv()
        opp_out[q, h] = both(q, h, FAR).astype(BF16)
        far_copy(q, h).start()

    last = (strips - 1, 1)

    def near_copies(q, h, way):
        device = to_down if way else to_up
        if (q, h) != last:
            return [remote(
                near_out.at[q, h, way], near_in.at[q, h, way],
                near_s.at[0], near_r.at[q, h, 0], device,
            )]
        return [
            remote(
                near_out.at[q, h, way, g], near_in.at[q, h, way, g],
                near_s.at[0], near_r.at[q, h, g], device,
            )
            for g in (1, 0)
        ]

    def send_near(q, h, way, v):
        near_out[q, h, way] = v.astype(BF16)
        for cp in near_copies(q, h, way):
            cp.start()

    def send_free(q, h):
        t = UP if h else DOWN
        core_copy(q, h, t).wait_recv()
        send_near(q, h, 1 - h, both(q, h, t))

    def send_joined(q, h):
        t = DOWN if h else UP
        core_copy(q, h, t).wait_recv()
        far_copy(q, h).wait_recv()
        send_near(q, h, h, both(q, h, t) + opp_in[q, h].astype(F32))

    def send_sum(q, h, g):
        remote(
            sum_out.at[q, h, g], sum_in.at[q, h, y], sum_s.at[0], sum_r.at[q, h],
            (after, c, d if g else across),
        ).start()

    def collect(q, h):
        core_copy(q, h, HERE).wait_recv()
        if (q, h) != last:
            remote(
                near_out.at[q, h], near_in.at[q, h], near_s.at[0], near_r.at[q, h, 0], to_up
            ).wait_recv()
            sum_out[q, h] = (
                both(q, h, HERE) + near_in[q, h, 0].astype(F32) + near_in[q, h, 1].astype(F32)
            ).astype(BF16)
            send_sum(q, h, 1)
            send_sum(q, h, 0)
            return
        for g in (1, 0):
            remote(
                near_out.at[q, h, :, g], near_in.at[q, h, :, g],
                near_s.at[0], near_r.at[q, h, g], to_up,
            ).wait_recv()
            sum_out[q, h, g] = (
                own[q, h, HERE, g] + core_in[q, h, HERE, g].astype(F32)
                + near_in[q, h, 0, g].astype(F32) + near_in[q, h, 1, g].astype(F32)
            ).astype(BF16)
            send_sum(q, h, g)

    def back_copy(k, q):
        i, device = member(k)
        return remote(
            back_out.at[q, i], back_in.at[q, me], back_s.at[q], back_r.at[q], device
        )

    def all_back_copies(q):
        block = pl.ds(0, MEMBERS - 1)
        return remote(
            back_out.at[q, block], back_in.at[q, block], back_s.at[q], back_r.at[q], to_core
        )

    sides = ((1 - y, CHIPS), (y, 0))

    def spread_rows(q, h, yy):
        final = (sum_in[q, h, 0].astype(F32) + sum_in[q, h, 1].astype(F32)).astype(BF16)
        at = pl.ds(pl.multiple_of(yy * (CHIPS * cap), CHIPS * cap), CHIPS * cap)
        return jnp.dot(
            place[at, h * half:(h + 1) * half], final, preferred_element_type=F32
        )

    def wait_sums(q, h):
        ref = sum_in.at[q, h]
        remote(ref, ref, sum_s.at[0], sum_r.at[q, h], to_core).wait_recv()

    def unpack_first(q):
        wait_sums(q, 0)
        for t, (yy, first) in enumerate(sides):
            partial[q % 2, t] = spread_rows(q, 0, yy)

    def unpack(q):
        wait_sums(q, 1)
        for t, (yy, first) in enumerate(sides):
            back_out[q, pl.ds(yy * CHIPS, CHIPS)] = (
                (partial[q % 2, t] + spread_rows(q, 1, yy))
                .astype(BF16)
                .reshape(CHIPS, cap, LANES)
            )
            for k in range(first + CHIPS - 1, max(first, 1) - 1, -1):
                back_copy(k, q).start()
        own_rows(q).start()

    def own_rows(q):
        return pltpu.make_async_copy(back_out.at[q, me], back_in.at[q, me], out_sem.at[q])

    activate(0)
    pltpu.make_async_copy(wd, wd, load_sem.at[2]).wait()
    project(0, 0, FAR, DOWN, UP)
    take_piece(far, 1, 1)
    take_piece(down, 1, 1)
    send_far(0, 0)
    send_free(0, 0)
    project(0, 0, HERE)
    project(1, 0, FAR, DOWN, UP)
    take_piece(afar, 1, 0)
    take_piece(adown, 1, 0)
    multiply(far, 1, 1)
    send_far(1, 0)
    send_free(1, 0)
    multiply(down, 1, 1)
    multiply(afar, 0, 1)
    multiply(adown, 0, 1)
    project(1, 0, HERE)
    project(2, 0, FAR, DOWN, UP)
    relay_on(3)
    take_piece(afar, 1, 1)
    take_piece(adown, 1, 1)
    send_far(2, 0)
    send_free(2, 0)
    project(2, 0, HERE)
    multiply(afar, 1, 1)
    multiply(adown, 1, 1)
    activate(1)
    send_joined(0, 0)
    project(0, 1, FAR, UP, DOWN)
    send_far(0, 1)
    project(0, 1, HERE)
    project(1, 1, FAR)
    send_joined(1, 0)
    send_free(0, 1)
    project(1, 1, UP, DOWN)
    send_far(1, 1)
    project(1, 1, HERE)
    project(2, 1, FAR)
    send_joined(2, 0)
    send_free(1, 1)
    project(2, 1, UP, DOWN)
    send_free(2, 1)
    project(2, 1, HERE)

    relay_counts.wait_recv()
    off = jnp.zeros((1, LANES), F32)
    s_i, r_i = iota((cap, rows), 0), iota((cap, rows), 1)
    for i in range(MEMBERS):
        n = counts_in[i].astype(F32)[0:1]
        hit = (r_i - s_i == off[:, 0:1]) & (s_i < n[:, 0:1])
        place[i * cap:(i + 1) * cap] = jnp.where(hit, 1.0, 0.0).astype(BF16)
        off = off + n

    collect(0, 0)
    send_joined(0, 1)
    send_far(2, 1)
    collect(1, 0)
    send_joined(1, 1)
    collect(0, 1)
    send_joined(2, 1)
    collect(2, 0)
    collect(1, 1)
    collect(2, 1)
    unpack_first(0)
    unpack(0)
    unpack_first(1)
    unpack_first(2)
    unpack(1)
    unpack(2)
    relay_route.wait_recv()
    relay_x = remote(x_mid, x_in, relay_s.at[3], relay_r.at[2], to_across)
    relay_x.wait_recv()
    for q in range(2):
        gather_sent(q)
    for src, dst, sem in (
        (core_out, core_in, core_s), (opp_out, opp_in, opp_s),
        (near_out, near_in, near_s), (sum_out, sum_in, sum_s),
    ):
        remote(src, dst, sem.at[0], relay_r.at[0], to_core).wait_send()
    relay_first = remote(x_v, x_mid, relay_s.at[2], mid_r.at[0], to_across)
    for cp in (relay_route, relay_counts, relay_first, relay_x):
        cp.wait_send()
    for q in range(strips):
        own_rows(q).wait()
        all_back_copies(q).wait_recv()
        all_back_copies(q).wait_send()


def finish(x_hbm, back_hbm, route_hbm, out_hbm, x_v, back_v, route_v, out_v, in_sem, out_sem):
    strips, owners, cap, lanes = back_v.shape
    part = strips * lanes
    width = x_v.shape[1] // FINISH_STEPS
    count = owners // FINISH_STEPS
    load_route = pltpu.make_async_copy(route_hbm, route_v, in_sem.at[0])
    load_route.start()
    loads, stores = [], []
    for i in range(FINISH_STEPS):
        at, ks = pl.ds(i * width, width), pl.ds(i * count, count)
        pair = (
            pltpu.make_async_copy(back_hbm.at[:, ks], back_v.at[:, ks], in_sem.at[1 + 2 * i]),
            pltpu.make_async_copy(x_hbm.at[:, at], x_v.at[:, at], in_sem.at[2 + 2 * i]),
        )
        for cp in pair:
            cp.start()
        loads.append(pair)
        stores.append(pltpu.make_async_copy(out_v.at[:, at], out_hbm.at[:, at], out_sem.at[i]))
    load_route.wait()
    spread = route_v[:, :cap].astype(BF16)
    weight = route_v[:, cap:cap + 1]
    for i in range(FINISH_STEPS):
        for cp in loads[i]:
            cp.wait()
        for k in range(i * count, (i + 1) * count):
            rows = jnp.concatenate([back_v[q, k] for q in range(strips)], axis=1)
            term = weight * jnp.dot(spread, rows, preferred_element_type=F32)
            at = slice(k * part, (k + 1) * part)
            out_v[:, at] = (x_v[:, at].astype(F32) + term).astype(BF16)
        stores[i].start()
    for cp in stores:
        cp.wait()


def solution(mesh):
    sections = mesh.shape["pipe"]

    def per_device(hidden_in, norm_gain, w_gate, w_up, w_down, expert_ids, gate_weights):
        tokens, width = hidden_in.shape
        ff = w_gate.shape[2]
        cap = tokens // 2
        rows = MEMBERS * cap // 2
        half = rows // 2
        part = width // MEMBERS
        strips = part // LANES
        vmem = pltpu.VMEM
        dma = pltpu.SemaphoreType.DMA
        any_space = pl.BlockSpec(memory_space=pl.ANY)
        x_in, back, route = pl.pallas_call(
            functools.partial(kernel, sections),
            out_shape=(
                jax.ShapeDtypeStruct((tokens, width), BF16),
                jax.ShapeDtypeStruct((strips, MEMBERS, cap, LANES), BF16),
                jax.ShapeDtypeStruct((tokens, tokens), F32),
            ),
            in_specs=[any_space] * 7,
            out_specs=(any_space,) * 3,
            scratch_shapes=[
                vmem((tokens, width), BF16),
                vmem((tokens, width), BF16),
                vmem((1, width), F32),
                vmem((2, tokens), jnp.int32),
                vmem((2, tokens), F32),
                vmem((tokens, tokens), F32),
                vmem((MEMBERS, TILE, LANES), BF16),
                vmem((MEMBERS, TILE, LANES), BF16),
                vmem((CHIPS, 2, part, ff), BF16),
                vmem((CHIPS, 2, part, ff), BF16),
                vmem((CHIPS, 2, ff, part), BF16),
                vmem((MEMBERS, cap + TILE, LANES), BF16),
                vmem((MEMBERS, cap, part - LANES), BF16),
                vmem((MEMBERS, cap + TILE, LANES), BF16),
                vmem((MEMBERS, cap, part - LANES), BF16),
                vmem((rows, MEMBERS * cap), BF16),
                vmem((MEMBERS * cap, rows), BF16),
                vmem((CHIPS * 4, half, LANES), BF16),
                vmem((CHIPS * 4, half, part - LANES), BF16),
                vmem((rows, ff), F32),
                vmem((rows, ff), F32),
                vmem((rows, ff), BF16),
                vmem((strips, 2, 4, 2, half, LANES), F32),
                vmem((strips, 2, 4, 2, half, LANES), BF16),
                vmem((strips, 2, 4, 2, half, LANES), BF16),
                vmem((strips, 2, 2, half, LANES), BF16),
                vmem((strips, 2, 2, half, LANES), BF16),
                vmem((strips, 2, 2, 2, half, LANES), BF16),
                vmem((strips, 2, 2, 2, half, LANES), BF16),
                vmem((strips, 2, 2, half, LANES), BF16),
                vmem((strips, 2, 2, half, LANES), BF16),
                vmem((2, 2, CHIPS * cap, LANES), F32),
                vmem((strips, MEMBERS, cap, LANES), BF16),
                dma((6 + X_LOADS,)), dma((strips,)),
                dma((2,)), dma((2,)),
                dma((2,)), dma((2, CHIPS, 2)), dma((2, CHIPS, 2)),
                dma((1,)), dma((strips, 2, 4)),
                dma((1,)), dma((strips, 2)),
                dma((1,)), dma((strips, 2, 2)),
                dma((1,)), dma((strips, 2)),
                dma((strips,)), dma((strips,)),
                dma((4,)), dma((3,)), dma((RELAY_PIECES,)),
            ],
            compiler_params=pltpu.CompilerParams(
                collective_id=0, has_side_effects=True, vmem_limit_bytes=62 * 2**20
            ),
            name="routed_block",
        )(
            hidden_in,
            norm_gain,
            w_gate.reshape(CHIPS, 2, part, ff),
            w_up.reshape(CHIPS, 2, part, ff),
            w_down.reshape(ff, width),
            expert_ids.T,
            gate_weights.T,
        )
        in_hbm = pl.BlockSpec(memory_space=pltpu.HBM)
        return pl.pallas_call(
            finish,
            out_shape=jax.ShapeDtypeStruct((tokens, width), BF16),
            in_specs=[in_hbm] * 3,
            out_specs=in_hbm,
            scratch_shapes=[
                vmem((tokens, width), BF16),
                vmem((strips, MEMBERS, cap, LANES), BF16),
                vmem((tokens, tokens), F32),
                vmem((tokens, width), BF16),
                dma((1 + 2 * FINISH_STEPS,)),
                dma((FINISH_STEPS,)),
            ],
            compiler_params=pltpu.CompilerParams(vmem_limit_bytes=62 * 2**20),
            name="add_rows",
        )(x_in, back, route)

    return jax.shard_map(
        per_device,
        mesh=mesh,
        in_specs=(
            P(("pipe", "expert", "dp"), None),
            P("pipe", None),
            P("pipe", None, ("expert", "dp")),
            P("pipe", None, ("expert", "dp")),
            P("pipe", ("expert", "dp"), None),
            P(("pipe", "expert", "dp"), None),
            P(("pipe", "expert", "dp"), None),
        ),
        out_specs=P(("pipe", "expert", "dp"), None),
        check_vma=False,
    )
```

```python
import functools

import jax
import jax.numpy as jnp
from jax import lax
from jax.experimental import pallas as pl
from jax.experimental.pallas import tpu as pltpu
from jax.sharding import PartitionSpec as P

MESH = pl.DeviceIdType.MESH
F32 = jnp.float32
BF16 = jnp.bfloat16
CHIPS = 8
MEMBERS = 16
LANES = 128
RELAY_PIECES = 4
X_LOADS = 4
FINISH_STEPS = 4
TILE = 16


def iota(shape, dim):
    return lax.broadcasted_iota(jnp.int32, shape, dim).astype(F32)


def kernel(
    sections,
    x_hbm, gain_hbm, wg_hbm, wu_hbm, wd_hbm, ids_hbm, gw_hbm,
    x_in, back_in, route_in,
    x_v, x_mid, gain, ids, gw, route, counts, counts_in, wg, wu, wd,
    packed_0, packed_1, slots_0, slots_1, pick, place, gath_0, gath_1, acc_g, acc_u, hid, own, core_out, core_in, opp_out, opp_in,
    near_out, near_in, sum_out, sum_in, partial, back_out,
    load_sem, out_sem, a2a_s, a2a_r, gath_s, gath_r, pair_r, core_s, core_r,
    opp_s, opp_r, near_s, near_r, sum_s, sum_r, back_s, back_r, relay_s, relay_r, mid_r,
):
    p, c, d = lax.axis_index("pipe"), lax.axis_index("expert"), lax.axis_index("dp")
    y, z = d // 4, d % 4
    me = d * 2 + c
    after, before = lax.rem(p + 1, sections), lax.rem(p + sections - 1, sections)
    tokens, width = x_v.shape
    packed, slots, gath = (packed_0, packed_1), (slots_0, slots_1), (gath_0, gath_1)
    cap = packed_1.shape[1]
    part = LANES + packed_1.shape[2]
    half = gath_0.shape[1]
    rows = 2 * half
    strips = part // LANES
    cuts = ((0, LANES), (LANES, part - LANES))

    def chip(other_y, step):
        yy = 1 - y if other_y else y
        return yy * 4 + (z + step) % 4

    up, down, across = chip(False, 1), chip(False, 3), chip(True, 0)
    to_up, to_down, to_across = (p, c, up), (p, c, down), (p, c, across)
    to_core = (p, 1 - c, d)

    def remote(src, dst, send, recv, device):
        return pltpu.make_async_remote_copy(
            src_ref=src, dst_ref=dst, send_sem=send, recv_sem=recv,
            device_id=device, device_id_type=MESH,
        )

    def loop(first, last, body):
        def step(k, carry):
            body(k)
            return carry

        lax.fori_loop(first, last, step, 0)

    def member(k):
        dd = (y + k // 8) % 2 * 4 + (z + k // 2) % 4
        e = (c + k) % 2
        return dd * 2 + e, (p, e, dd)

    block = width // X_LOADS
    loads_x = [
        pltpu.make_async_copy(
            x_hbm.at[:, pl.ds(n * block, block)], x_v.at[:, pl.ds(n * block, block)],
            load_sem.at[6 + n],
        )
        for n in range(X_LOADS)
    ]
    load_g = pltpu.make_async_copy(wg_hbm, wg, load_sem.at[0])
    load_u = pltpu.make_async_copy(wu_hbm, wu, load_sem.at[1])
    small = [
        pltpu.make_async_copy(src, dst, load_sem.at[3 + n])
        for n, (src, dst) in enumerate(((ids_hbm, ids), (gw_hbm, gw), (gain_hbm, gain)))
    ]
    small[0].start()
    small[1].start()
    for cp in loads_x:
        cp.start()
    small[2].start()

    barrier = pltpu.get_barrier_semaphore()

    def greet(device):
        pl.semaphore_signal(barrier, inc=1, device_id=device, device_id_type=MESH)

    loop(1, MEMBERS, lambda k: greet(member(k)[1]))
    greet((before, c, d))
    greet((before, c, across))

    small[0].wait()
    small[1].wait()
    square = (tokens, tokens)
    chosen = ids[...] == 0
    routed = jnp.max(jnp.where(chosen, 1.0, 0.0), axis=0, keepdims=True)
    weight = jnp.sum(jnp.where(chosen, gw[...], 0.0), axis=0, keepdims=True)
    routed_b = jnp.broadcast_to(routed, square)
    tri = jnp.where(iota(square, 0) <= iota(square, 1), 1.0, 0.0).astype(BF16)
    rank = jnp.dot(routed_b.astype(BF16), tri, preferred_element_type=F32)
    spot = jnp.where((routed_b > 0.5) & (rank - 1.0 == iota(square, 0)), 1.0, 0.0)
    spot_t = spot[:cap].astype(BF16)
    route[...] = jnp.where(
        iota(square, 1) < cap, spot.T, jnp.broadcast_to(weight, square).T
    )
    count = jnp.dot(
        routed_b[:TILE].astype(BF16), jnp.ones(square, BF16), preferred_element_type=F32
    ).astype(BF16)
    for i in range(MEMBERS):
        packed_0[i, cap:] = count

    total = jnp.zeros((tokens, LANES), F32)
    for n, cp in enumerate(loads_x):
        cp.wait()
        for t in range(block // LANES):
            start = n * block + t * LANES
            v = x_v[:, start:start + LANES].astype(F32)
            total = total + v * v
    scale = lax.rsqrt(jnp.sum(total, axis=1, keepdims=True) / width + 1e-05)
    small[2].wait()
    load_g.start()
    load_u.start()
    for j in range(CHIPS):
        for e in range(2):
            pltpu.make_async_copy(
                wd_hbm.at[:, pl.ds((2 * j + e) * part, part)], wd.at[j, e], load_sem.at[2]
            ).start()

    def pack(j, q):
        start, size = cuts[q]
        for t in range(4):
            i = j * 4 + t
            offset = i * part + start
            if not isinstance(j, int):
                offset = pl.multiple_of(offset, LANES)
            at = pl.ds(offset, size)
            n = (x_v[:, at].astype(F32) * scale * gain[:, at]).astype(BF16)
            packed[q][i, :cap] = jnp.dot(
                spot_t, n, preferred_element_type=F32
            ).astype(BF16)

    for j in range(MEMBERS // 4):
        pack(j, 0)
    pl.semaphore_wait(barrier, MEMBERS + 1)

    def slot_copy(k, q):
        i, device = member(k)
        return remote(
            packed[q].at[i], slots[q].at[me], a2a_s.at[q], a2a_r.at[q], device
        )

    def all_slot_copies(q):
        block = pl.ds(0, MEMBERS - 1)
        return remote(
            packed[q].at[block], slots[q].at[block], a2a_s.at[q], a2a_r.at[q], to_core
        )

    for k in range(MEMBERS - 1, 0, -1):
        slot_copy(k, 0).start()
    loop(0, MEMBERS // 4, lambda j: pack(j, 1))
    for k in range(MEMBERS - 1, 0, -1):
        slot_copy(k, 1).start()

    def relay_piece(i):
        at = pl.ds(i * (tokens // RELAY_PIECES), tokens // RELAY_PIECES)
        return remote(
            x_v.at[at], x_mid.at[at], relay_s.at[2], mid_r.at[i], (after, c, across)
        )

    def relay_on(i):
        relay_piece(i).wait_recv()
        at = pl.ds(i * (tokens // RELAY_PIECES), tokens // RELAY_PIECES)
        remote(x_mid.at[at], x_in.at[at], relay_s.at[3], relay_r.at[2], to_across).start()

    for i in range(RELAY_PIECES):
        relay_piece(i).start()
    for q in range(2):
        slots[q][me] = packed[q][me]
    all_slot_copies(0).wait_recv()
    counts[...] = slots_0[:, cap:]
    counterpart = (after, c, d)
    relay_route = remote(route, route_in, relay_s.at[0], relay_r.at[0], counterpart)
    relay_route.start()
    relay_counts = remote(counts, counts_in, relay_s.at[1], relay_r.at[1], counterpart)
    relay_counts.start()

    off = jnp.zeros((1, LANES), F32)
    lane1 = iota((1, LANES), 1)
    high = lane1 - cap
    row_i = iota((rows, LANES), 0)
    for q in range(MEMBERS // 2):
        n0, n1 = counts[2 * q].astype(F32)[0:1], counts[2 * q + 1].astype(F32)[0:1]
        target = jnp.where(
            lane1 < cap,
            jnp.where(lane1 < n0, off + lane1, -1.0),
            jnp.where(high < n1, off + n0 + high, -1.0),
        )
        pick[:, q * LANES:(q + 1) * LANES] = jnp.where(row_i == target, 1.0, 0.0).astype(BF16)
        off = off + n0 + n1

    sends = [0, 0]

    def spot_of(j, e, h):
        return (j * 2 + e) * 2 + h

    def send_piece(j, h, q, *devices):
        ref = gath[q].at[spot_of(j, c, h)]
        for device in devices:
            sem = (pair_r if device is to_core else gath_r).at[q, j, h]
            remote(ref, ref, gath_s.at[q], sem, device).start()
            sends[q] += 1

    def take_piece(j, h, q, *devices):
        ref = gath[q].at[spot_of(j, c, h)]
        remote(ref, ref, gath_s.at[q], gath_r.at[q, j, h], to_core).wait_recv()
        send_piece(j, h, q, *devices, to_core)

    def gather_sent(q):
        ref = gath[q].at[pl.ds(0, sends[q])]
        remote(ref, ref, gath_s.at[q], gath_r.at[q, 0, 0], to_core).wait_send()

    def multiply(j, q, h, first=False):
        other = gath[q].at[spot_of(j, 1 - c, h)]
        remote(other, other, gath_s.at[q], pair_r.at[q, j, h], to_core).wait_recv()
        start, size = cuts[q]
        cols = slice(start, start + size)
        at = slice(h * half, (h + 1) * half)
        a = jnp.concatenate([gath[q][spot_of(j, e, h)] for e in range(2)], axis=1)
        for w, acc in ((wg, acc_g), (wu, acc_u)):
            b = jnp.concatenate([w[j, e, cols] for e in range(2)], axis=0)
            v = jnp.dot(a, b, preferred_element_type=F32)
            if first:
                acc[at] = v
            else:
                acc[at] += v

    for q, (start, size) in enumerate(cuts):
        if q:
            all_slot_copies(q).wait_recv()
        all_slots = slots[q][:, :cap].reshape(MEMBERS * cap, size)
        for h in range(2):
            gath[q][spot_of(d, c, h)] = jnp.dot(
                pick[h * half:(h + 1) * half], all_slots, preferred_element_type=F32
            ).astype(BF16)
            if h == 0 or q == 0:
                send_piece(d, h, q, to_up)
            send_piece(d, h, q, to_down, to_across, to_core)

    aup, adown, far, afar = chip(True, 1), chip(True, 3), chip(False, 2), chip(True, 2)
    load_g.wait()
    load_u.wait()
    multiply(d, 0, 0, first=True)
    multiply(d, 0, 1, first=True)
    take_piece(down, 0, 0, to_up)
    take_piece(up, 1, 0, to_down)
    take_piece(up, 0, 0)
    take_piece(down, 1, 0)
    multiply(d, 1, 0)
    multiply(d, 1, 1)
    take_piece(across, 0, 0, to_up, to_down)
    take_piece(across, 1, 0, to_down)
    multiply(down, 0, 0)
    multiply(up, 0, 0)
    take_piece(across, 0, 1, to_up, to_down)
    take_piece(down, 0, 1, to_up)
    take_piece(up, 0, 1)
    multiply(across, 0, 0)
    multiply(across, 0, 1)
    multiply(down, 0, 1)
    multiply(up, 0, 1)
    take_piece(across, 1, 1, to_down)
    relay_on(0)
    for q in range(2):
        all_slot_copies(q).wait_send()
    take_piece(adown, 0, 0, to_up)
    take_piece(up, 1, 1, to_down)
    take_piece(far, 0, 0)
    multiply(across, 1, 0)
    multiply(down, 1, 0)
    multiply(up, 1, 0)
    multiply(far, 0, 0)

    take_piece(aup, 0, 0)
    take_piece(adown, 0, 1, to_up)
    send_piece(d, 1, 1, to_up)
    send_piece(across, 1, 0, to_up)
    send_piece(across, 1, 1, to_up)
    multiply(up, 1, 1)
    take_piece(aup, 1, 0, to_down)
    take_piece(far, 1, 0)
    multiply(across, 1, 1)
    multiply(adown, 0, 0)
    multiply(aup, 0, 0)
    multiply(adown, 1, 0)
    multiply(far, 0, 1)
    multiply(aup, 0, 1)
    relay_on(1)
    take_piece(far, 0, 1)
    take_piece(aup, 0, 1)
    take_piece(afar, 0, 0)
    multiply(far, 1, 0)
    multiply(aup, 1, 0)
    take_piece(aup, 1, 1, to_down)
    multiply(afar, 0, 0)
    take_piece(afar, 0, 1)
    multiply(aup, 1, 1)
    multiply(afar, 1, 0)

    def activate(h):
        def block(n):
            at = pl.ds(pl.multiple_of(h * half + n * 128, 128), 128)
            g = acc_g[at]
            hid[at] = (g / (1.0 + jnp.exp(-g)) * acc_u[at]).astype(BF16)

        loop(0, half // 128, block)

    FAR, UP, DOWN, HERE = range(4)
    steps = (2, 1, 3, 0)

    def core_copy(q, h, t):
        return remote(
            core_out.at[q, h, t], core_in.at[q, h, t], core_s.at[0], core_r.at[q, h, t], to_core
        )

    def project(q, h, *targets):
        cols = slice(q * LANES, (q + 1) * LANES)
        for t in targets:
            chips = (chip(True, steps[t]), chip(False, steps[t]))
            w = jnp.concatenate(
                [wd[j, e, :, cols] for j in chips for e in (1 - c, c)], axis=1
            )
            v = jnp.dot(hid[h * half:(h + 1) * half], w, preferred_element_type=F32)
            for g in range(2):
                core_out[q, h, t, g] = v[:, 2 * g * LANES:(2 * g + 1) * LANES].astype(BF16)
                own[q, h, t, g] = v[:, (2 * g + 1) * LANES:(2 * g + 2) * LANES]
            core_copy(q, h, t).start()

    def both(q, h, t):
        return own[q, h, t] + core_in[q, h, t].astype(F32)

    def far_copy(q, h):
        return remote(
            opp_out.at[q, h], opp_in.at[q, h], opp_s.at[0], opp_r.at[q, h],
            to_down if h else to_up,
        )

    def send_far(q, h):
        core_copy(q, h, FAR).wait_recv()
        opp_out[q, h] = both(q, h, FAR).astype(BF16)
        far_copy(q, h).start()

    last = (strips - 1, 1)

    def near_copies(q, h, way):
        device = to_down if way else to_up
        if (q, h) != last:
            return [remote(
                near_out.at[q, h, way], near_in.at[q, h, way],
                near_s.at[0], near_r.at[q, h, 0], device,
            )]
        return [
            remote(
                near_out.at[q, h, way, g], near_in.at[q, h, way, g],
                near_s.at[0], near_r.at[q, h, g], device,
            )
            for g in (1, 0)
        ]

    def send_near(q, h, way, v):
        near_out[q, h, way] = v.astype(BF16)
        for cp in near_copies(q, h, way):
            cp.start()

    def send_free(q, h):
        t = UP if h else DOWN
        core_copy(q, h, t).wait_recv()
        send_near(q, h, 1 - h, both(q, h, t))

    def send_joined(q, h):
        t = DOWN if h else UP
        core_copy(q, h, t).wait_recv()
        far_copy(q, h).wait_recv()
        send_near(q, h, h, both(q, h, t) + opp_in[q, h].astype(F32))

    def send_sum(q, h, g):
        remote(
            sum_out.at[q, h, g], sum_in.at[q, h, y], sum_s.at[0], sum_r.at[q, h],
            (after, c, d if g else across),
        ).start()

    def collect(q, h):
        core_copy(q, h, HERE).wait_recv()
        if (q, h) != last:
            remote(
                near_out.at[q, h], near_in.at[q, h], near_s.at[0], near_r.at[q, h, 0], to_up
            ).wait_recv()
            sum_out[q, h] = (
                both(q, h, HERE) + near_in[q, h, 0].astype(F32) + near_in[q, h, 1].astype(F32)
            ).astype(BF16)
            send_sum(q, h, 1)
            send_sum(q, h, 0)
            return
        for g in (1, 0):
            remote(
                near_out.at[q, h, :, g], near_in.at[q, h, :, g],
                near_s.at[0], near_r.at[q, h, g], to_up,
            ).wait_recv()
            sum_out[q, h, g] = (
                own[q, h, HERE, g] + core_in[q, h, HERE, g].astype(F32)
                + near_in[q, h, 0, g].astype(F32) + near_in[q, h, 1, g].astype(F32)
            ).astype(BF16)
            send_sum(q, h, g)

    def back_copy(k, q):
        i, device = member(k)
        return remote(
            back_out.at[q, i], back_in.at[q, me], back_s.at[q], back_r.at[q], device
        )

    def all_back_copies(q):
        block = pl.ds(0, MEMBERS - 1)
        return remote(
            back_out.at[q, block], back_in.at[q, block], back_s.at[q], back_r.at[q], to_core
        )

    sides = ((1 - y, CHIPS), (y, 0))

    def spread_rows(q, h, yy):
        final = (sum_in[q, h, 0].astype(F32) + sum_in[q, h, 1].astype(F32)).astype(BF16)
        at = pl.ds(pl.multiple_of(yy * (CHIPS * cap), CHIPS * cap), CHIPS * cap)
        return jnp.dot(
            place[at, h * half:(h + 1) * half], final, preferred_element_type=F32
        )

    def wait_sums(q, h):
        ref = sum_in.at[q, h]
        remote(ref, ref, sum_s.at[0], sum_r.at[q, h], to_core).wait_recv()

    def unpack_first(q):
        wait_sums(q, 0)
        for t, (yy, first) in enumerate(sides):
            partial[q % 2, t] = spread_rows(q, 0, yy)

    def unpack(q):
        wait_sums(q, 1)
        for t, (yy, first) in enumerate(sides):
            back_out[q, pl.ds(yy * CHIPS, CHIPS)] = (
                (partial[q % 2, t] + spread_rows(q, 1, yy))
                .astype(BF16)
                .reshape(CHIPS, cap, LANES)
            )
            for k in range(first + CHIPS - 1, max(first, 1) - 1, -1):
                back_copy(k, q).start()
        own_rows(q).start()

    def own_rows(q):
        return pltpu.make_async_copy(back_out.at[q, me], back_in.at[q, me], out_sem.at[q])

    activate(0)
    pltpu.make_async_copy(wd, wd, load_sem.at[2]).wait()
    project(0, 0, FAR, DOWN, UP)
    take_piece(far, 1, 1)
    take_piece(down, 1, 1)
    send_far(0, 0)
    send_free(0, 0)
    project(0, 0, HERE)
    relay_on(2)
    project(1, 0, FAR, DOWN, UP)
    take_piece(afar, 1, 0)
    take_piece(adown, 1, 0)
    multiply(far, 1, 1)
    send_far(1, 0)
    send_free(1, 0)
    multiply(down, 1, 1)
    multiply(afar, 0, 1)
    multiply(adown, 0, 1)
    project(1, 0, HERE)
    project(2, 0, FAR, DOWN, UP)
    take_piece(afar, 1, 1)
    take_piece(adown, 1, 1)
    send_far(2, 0)
    send_free(2, 0)
    project(2, 0, HERE)
    relay_on(3)
    multiply(afar, 1, 1)
    multiply(adown, 1, 1)
    activate(1)
    send_joined(0, 0)
    project(0, 1, FAR, UP, DOWN)
    send_far(0, 1)
    project(0, 1, HERE)
    project(1, 1, FAR)
    send_joined(1, 0)
    send_free(0, 1)
    project(1, 1, UP, DOWN)
    send_far(1, 1)
    project(1, 1, HERE)
    project(2, 1, FAR)
    send_joined(2, 0)
    send_free(1, 1)
    project(2, 1, UP, DOWN)
    send_free(2, 1)
    project(2, 1, HERE)

    relay_counts.wait_recv()
    off = jnp.zeros((1, LANES), F32)
    s_i, r_i = iota((cap, rows), 0), iota((cap, rows), 1)
    for i in range(MEMBERS):
        n = counts_in[i].astype(F32)[0:1]
        hit = (r_i - s_i == off[:, 0:1]) & (s_i < n[:, 0:1])
        place[i * cap:(i + 1) * cap] = jnp.where(hit, 1.0, 0.0).astype(BF16)
        off = off + n

    collect(0, 0)
    send_joined(0, 1)
    send_far(2, 1)
    collect(1, 0)
    send_joined(1, 1)
    collect(0, 1)
    send_joined(2, 1)
    collect(2, 0)
    collect(1, 1)
    collect(2, 1)
    unpack_first(0)
    unpack(0)
    unpack_first(1)
    unpack_first(2)
    unpack(1)
    unpack(2)
    relay_route.wait_recv()
    relay_x = remote(x_mid, x_in, relay_s.at[3], relay_r.at[2], to_across)
    relay_x.wait_recv()
    for q in range(2):
        gather_sent(q)
    for src, dst, sem in (
        (core_out, core_in, core_s), (opp_out, opp_in, opp_s),
        (near_out, near_in, near_s), (sum_out, sum_in, sum_s),
    ):
        remote(src, dst, sem.at[0], relay_r.at[0], to_core).wait_send()
    relay_first = remote(x_v, x_mid, relay_s.at[2], mid_r.at[0], to_across)
    for cp in (relay_route, relay_counts, relay_first, relay_x):
        cp.wait_send()
    for q in range(strips):
        own_rows(q).wait()
        all_back_copies(q).wait_recv()
        all_back_copies(q).wait_send()


def finish(x_hbm, back_hbm, route_hbm, out_hbm, x_v, back_v, route_v, out_v, in_sem, out_sem):
    strips, owners, cap, lanes = back_v.shape
    part = strips * lanes
    width = x_v.shape[1] // FINISH_STEPS
    count = owners // FINISH_STEPS
    load_route = pltpu.make_async_copy(route_hbm, route_v, in_sem.at[0])
    load_route.start()
    loads, stores = [], []
    for i in range(FINISH_STEPS):
        at, ks = pl.ds(i * width, width), pl.ds(i * count, count)
        pair = (
            pltpu.make_async_copy(back_hbm.at[:, ks], back_v.at[:, ks], in_sem.at[1 + 2 * i]),
            pltpu.make_async_copy(x_hbm.at[:, at], x_v.at[:, at], in_sem.at[2 + 2 * i]),
        )
        for cp in pair:
            cp.start()
        loads.append(pair)
        stores.append(pltpu.make_async_copy(out_v.at[:, at], out_hbm.at[:, at], out_sem.at[i]))
    load_route.wait()
    spread = route_v[:, :cap].astype(BF16)
    weight = route_v[:, cap:cap + 1]
    for i in range(FINISH_STEPS):
        for cp in loads[i]:
            cp.wait()
        for k in range(i * count, (i + 1) * count):
            rows = jnp.concatenate([back_v[q, k] for q in range(strips)], axis=1)
            term = weight * jnp.dot(spread, rows, preferred_element_type=F32)
            at = slice(k * part, (k + 1) * part)
            out_v[:, at] = (x_v[:, at].astype(F32) + term).astype(BF16)
        stores[i].start()
    for cp in stores:
        cp.wait()


def solution(mesh):
    sections = mesh.shape["pipe"]

    def per_device(hidden_in, norm_gain, w_gate, w_up, w_down, expert_ids, gate_weights):
        tokens, width = hidden_in.shape
        ff = w_gate.shape[2]
        cap = tokens // 2
        rows = MEMBERS * cap // 2
        half = rows // 2
        part = width // MEMBERS
        strips = part // LANES
        vmem = pltpu.VMEM
        dma = pltpu.SemaphoreType.DMA
        any_space = pl.BlockSpec(memory_space=pl.ANY)
        x_in, back, route = pl.pallas_call(
            functools.partial(kernel, sections),
            out_shape=(
                jax.ShapeDtypeStruct((tokens, width), BF16),
                jax.ShapeDtypeStruct((strips, MEMBERS, cap, LANES), BF16),
                jax.ShapeDtypeStruct((tokens, tokens), F32),
            ),
            in_specs=[any_space] * 7,
            out_specs=(any_space,) * 3,
            scratch_shapes=[
                vmem((tokens, width), BF16),
                vmem((tokens, width), BF16),
                vmem((1, width), F32),
                vmem((2, tokens), jnp.int32),
                vmem((2, tokens), F32),
                vmem((tokens, tokens), F32),
                vmem((MEMBERS, TILE, LANES), BF16),
                vmem((MEMBERS, TILE, LANES), BF16),
                vmem((CHIPS, 2, part, ff), BF16),
                vmem((CHIPS, 2, part, ff), BF16),
                vmem((CHIPS, 2, ff, part), BF16),
                vmem((MEMBERS, cap + TILE, LANES), BF16),
                vmem((MEMBERS, cap, part - LANES), BF16),
                vmem((MEMBERS, cap + TILE, LANES), BF16),
                vmem((MEMBERS, cap, part - LANES), BF16),
                vmem((rows, MEMBERS * cap), BF16),
                vmem((MEMBERS * cap, rows), BF16),
                vmem((CHIPS * 4, half, LANES), BF16),
                vmem((CHIPS * 4, half, part - LANES), BF16),
                vmem((rows, ff), F32),
                vmem((rows, ff), F32),
                vmem((rows, ff), BF16),
                vmem((strips, 2, 4, 2, half, LANES), F32),
                vmem((strips, 2, 4, 2, half, LANES), BF16),
                vmem((strips, 2, 4, 2, half, LANES), BF16),
                vmem((strips, 2, 2, half, LANES), BF16),
                vmem((strips, 2, 2, half, LANES), BF16),
                vmem((strips, 2, 2, 2, half, LANES), BF16),
                vmem((strips, 2, 2, 2, half, LANES), BF16),
                vmem((strips, 2, 2, half, LANES), BF16),
                vmem((strips, 2, 2, half, LANES), BF16),
                vmem((2, 2, CHIPS * cap, LANES), F32),
                vmem((strips, MEMBERS, cap, LANES), BF16),
                dma((6 + X_LOADS,)), dma((strips,)),
                dma((2,)), dma((2,)),
                dma((2,)), dma((2, CHIPS, 2)), dma((2, CHIPS, 2)),
                dma((1,)), dma((strips, 2, 4)),
                dma((1,)), dma((strips, 2)),
                dma((1,)), dma((strips, 2, 2)),
                dma((1,)), dma((strips, 2)),
                dma((strips,)), dma((strips,)),
                dma((4,)), dma((3,)), dma((RELAY_PIECES,)),
            ],
            compiler_params=pltpu.CompilerParams(
                collective_id=0, has_side_effects=True, vmem_limit_bytes=62 * 2**20
            ),
            name="routed_block",
        )(
            hidden_in,
            norm_gain,
            w_gate.reshape(CHIPS, 2, part, ff),
            w_up.reshape(CHIPS, 2, part, ff),
            w_down.reshape(ff, width),
            expert_ids.T,
            gate_weights.T,
        )
        in_hbm = pl.BlockSpec(memory_space=pltpu.HBM)
        return pl.pallas_call(
            finish,
            out_shape=jax.ShapeDtypeStruct((tokens, width), BF16),
            in_specs=[in_hbm] * 3,
            out_specs=in_hbm,
            scratch_shapes=[
                vmem((tokens, width), BF16),
                vmem((strips, MEMBERS, cap, LANES), BF16),
                vmem((tokens, tokens), F32),
                vmem((tokens, width), BF16),
                dma((1 + 2 * FINISH_STEPS,)),
                dma((FINISH_STEPS,)),
            ],
            compiler_params=pltpu.CompilerParams(vmem_limit_bytes=62 * 2**20),
            name="add_rows",
        )(x_in, back, route)

    return jax.shard_map(
        per_device,
        mesh=mesh,
        in_specs=(
            P(("pipe", "expert", "dp"), None),
            P("pipe", None),
            P("pipe", None, ("expert", "dp")),
            P("pipe", None, ("expert", "dp")),
            P("pipe", ("expert", "dp"), None),
            P(("pipe", "expert", "dp"), None),
            P(("pipe", "expert", "dp"), None),
        ),
        out_specs=P(("pipe", "expert", "dp"), None),
        check_vma=False,
    )
```

```python
import functools

import jax
import jax.numpy as jnp
from jax import lax
from jax.experimental import pallas as pl
from jax.experimental.pallas import tpu as pltpu
from jax.sharding import PartitionSpec as P

MESH = pl.DeviceIdType.MESH
F32 = jnp.float32
BF16 = jnp.bfloat16
CHIPS = 8
MEMBERS = 16
LANES = 128
RELAY_PIECES = 4
X_LOADS = 4
FINISH_STEPS = 2
TILE = 16


def iota(shape, dim):
    return lax.broadcasted_iota(jnp.int32, shape, dim).astype(F32)


def kernel(
    sections,
    x_hbm, gain_hbm, wg_hbm, wu_hbm, wd_hbm, ids_hbm, gw_hbm,
    x_in, back_in, route_in,
    x_v, x_mid, gain, ids, gw, route, counts, counts_in, wg, wu, wd,
    packed_0, packed_1, slots_0, slots_1, pick, place, gath_0, gath_1, acc_g, acc_u, hid, own, core_out, core_in, opp_out, opp_in,
    near_out, near_in, sum_out, sum_in, partial, back_out,
    load_sem, out_sem, a2a_s, a2a_r, gath_s, gath_r, pair_r, core_s, core_r,
    opp_s, opp_r, near_s, near_r, sum_s, sum_r, back_s, back_r, relay_s, relay_r, mid_r,
):
    p, c, d = lax.axis_index("pipe"), lax.axis_index("expert"), lax.axis_index("dp")
    y, z = d // 4, d % 4
    me = d * 2 + c
    after, before = lax.rem(p + 1, sections), lax.rem(p + sections - 1, sections)
    tokens, width = x_v.shape
    packed, slots, gath = (packed_0, packed_1), (slots_0, slots_1), (gath_0, gath_1)
    cap = packed_1.shape[1]
    part = LANES + packed_1.shape[2]
    half = gath_0.shape[1]
    rows = 2 * half
    strips = part // LANES
    cuts = ((0, LANES), (LANES, part - LANES))

    def chip(other_y, step):
        yy = 1 - y if other_y else y
        return yy * 4 + (z + step) % 4

    up, down, across = chip(False, 1), chip(False, 3), chip(True, 0)
    to_up, to_down, to_across = (p, c, up), (p, c, down), (p, c, across)
    to_core = (p, 1 - c, d)

    def remote(src, dst, send, recv, device):
        return pltpu.make_async_remote_copy(
            src_ref=src, dst_ref=dst, send_sem=send, recv_sem=recv,
            device_id=device, device_id_type=MESH,
        )

    def loop(first, last, body):
        def step(k, carry):
            body(k)
            return carry

        lax.fori_loop(first, last, step, 0)

    def member(k):
        dd = (y + k // 8) % 2 * 4 + (z + k // 2) % 4
        e = (c + k) % 2
        return dd * 2 + e, (p, e, dd)

    block = width // X_LOADS
    loads_x = [
        pltpu.make_async_copy(
            x_hbm.at[:, pl.ds(n * block, block)], x_v.at[:, pl.ds(n * block, block)],
            load_sem.at[6 + n],
        )
        for n in range(X_LOADS)
    ]
    load_g = pltpu.make_async_copy(wg_hbm, wg, load_sem.at[0])
    load_u = pltpu.make_async_copy(wu_hbm, wu, load_sem.at[1])
    small = [
        pltpu.make_async_copy(src, dst, load_sem.at[3 + n])
        for n, (src, dst) in enumerate(((ids_hbm, ids), (gw_hbm, gw), (gain_hbm, gain)))
    ]
    small[0].start()
    small[1].start()
    for cp in loads_x:
        cp.start()
    small[2].start()

    barrier = pltpu.get_barrier_semaphore()

    def greet(device):
        pl.semaphore_signal(barrier, inc=1, device_id=device, device_id_type=MESH)

    greet((before, c, d))
    greet((before, c, across))
    for k in range(MEMBERS - 1, 0, -1):
        greet(member(k)[1])

    small[0].wait()
    small[1].wait()
    square = (tokens, tokens)
    chosen = ids[...] == 0
    routed = jnp.max(jnp.where(chosen, 1.0, 0.0), axis=0, keepdims=True)
    weight = jnp.sum(jnp.where(chosen, gw[...], 0.0), axis=0, keepdims=True)
    routed_b = jnp.broadcast_to(routed, square)
    tri = jnp.where(iota(square, 0) <= iota(square, 1), 1.0, 0.0).astype(BF16)
    rank = jnp.dot(routed_b.astype(BF16), tri, preferred_element_type=F32)
    spot = jnp.where((routed_b > 0.5) & (rank - 1.0 == iota(square, 0)), 1.0, 0.0)
    spot_t = spot[:cap].astype(BF16)
    route[...] = jnp.where(
        iota(square, 1) < cap, spot.T, jnp.broadcast_to(weight, square).T
    )
    count = jnp.dot(
        routed_b[:TILE].astype(BF16), jnp.ones(square, BF16), preferred_element_type=F32
    ).astype(BF16)
    for i in range(MEMBERS):
        packed_0[i, cap:] = count

    total = jnp.zeros((tokens, LANES), F32)
    for n, cp in enumerate(loads_x):
        cp.wait()
        for t in range(block // LANES):
            start = n * block + t * LANES
            v = x_v[:, start:start + LANES].astype(F32)
            total = total + v * v
    scale = lax.rsqrt(jnp.sum(total, axis=1, keepdims=True) / width + 1e-05)
    small[2].wait()
    load_g.start()
    load_u.start()
    for j in range(CHIPS):
        for e in range(2):
            pltpu.make_async_copy(
                wd_hbm.at[:, pl.ds((2 * j + e) * part, part)], wd.at[j, e], load_sem.at[2]
            ).start()

    def pack(j, q):
        start, size = cuts[q]
        for t in range(4):
            i = j * 4 + t
            offset = i * part + start
            if not isinstance(j, int):
                offset = pl.multiple_of(offset, LANES)
            at = pl.ds(offset, size)
            n = (x_v[:, at].astype(F32) * scale * gain[:, at]).astype(BF16)
            packed[q][i, :cap] = jnp.dot(
                spot_t, n, preferred_element_type=F32
            ).astype(BF16)

    for j in range(MEMBERS // 4):
        pack(j, 0)
    pl.semaphore_wait(barrier, MEMBERS + 1)

    def slot_copy(k, q):
        i, device = member(k)
        return remote(
            packed[q].at[i], slots[q].at[me], a2a_s.at[q], a2a_r.at[q], device
        )

    def all_slot_copies(q):
        block = pl.ds(0, MEMBERS - 1)
        return remote(
            packed[q].at[block], slots[q].at[block], a2a_s.at[q], a2a_r.at[q], to_core
        )

    for k in range(MEMBERS - 1, 0, -1):
        slot_copy(k, 0).start()
    loop(0, MEMBERS // 4, lambda j: pack(j, 1))
    for k in range(MEMBERS - 1, 0, -1):
        slot_copy(k, 1).start()

    def relay_piece(i):
        at = pl.ds(i * (tokens // RELAY_PIECES), tokens // RELAY_PIECES)
        return remote(
            x_v.at[at], x_mid.at[at], relay_s.at[2], mid_r.at[i], (after, c, across)
        )

    def relay_on(i):
        relay_piece(i).wait_recv()
        at = pl.ds(i * (tokens // RELAY_PIECES), tokens // RELAY_PIECES)
        remote(x_mid.at[at], x_in.at[at], relay_s.at[3], relay_r.at[2], to_across).start()

    for i in range(RELAY_PIECES):
        relay_piece(i).start()
    for q in range(2):
        slots[q][me] = packed[q][me]
    all_slot_copies(0).wait_recv()
    counts[...] = slots_0[:, cap:]
    counterpart = (after, c, d)
    relay_route = remote(route, route_in, relay_s.at[0], relay_r.at[0], counterpart)
    relay_route.start()
    relay_counts = remote(counts, counts_in, relay_s.at[1], relay_r.at[1], counterpart)
    relay_counts.start()

    off = jnp.zeros((1, LANES), F32)
    lane1 = iota((1, LANES), 1)
    high = lane1 - cap
    row_i = iota((rows, LANES), 0)
    for q in range(MEMBERS // 2):
        n0, n1 = counts[2 * q].astype(F32)[0:1], counts[2 * q + 1].astype(F32)[0:1]
        target = jnp.where(
            lane1 < cap,
            jnp.where(lane1 < n0, off + lane1, -1.0),
            jnp.where(high < n1, off + n0 + high, -1.0),
        )
        pick[:, q * LANES:(q + 1) * LANES] = jnp.where(row_i == target, 1.0, 0.0).astype(BF16)
        off = off + n0 + n1

    sends = [0, 0]

    def spot_of(j, e, h):
        return (j * 2 + e) * 2 + h

    def send_piece(j, h, q, *devices):
        ref = gath[q].at[spot_of(j, c, h)]
        for device in devices:
            sem = (pair_r if device is to_core else gath_r).at[q, j, h]
            remote(ref, ref, gath_s.at[q], sem, device).start()
            sends[q] += 1

    def take_piece(j, h, q, *devices):
        ref = gath[q].at[spot_of(j, c, h)]
        remote(ref, ref, gath_s.at[q], gath_r.at[q, j, h], to_core).wait_recv()
        send_piece(j, h, q, *devices, to_core)

    def gather_sent(q):
        ref = gath[q].at[pl.ds(0, sends[q])]
        remote(ref, ref, gath_s.at[q], gath_r.at[q, 0, 0], to_core).wait_send()

    def multiply(j, q, h, first=False):
        other = gath[q].at[spot_of(j, 1 - c, h)]
        remote(other, other, gath_s.at[q], pair_r.at[q, j, h], to_core).wait_recv()
        start, size = cuts[q]
        cols = slice(start, start + size)
        at = slice(h * half, (h + 1) * half)
        a = jnp.concatenate([gath[q][spot_of(j, e, h)] for e in range(2)], axis=1)
        for w, acc in ((wg, acc_g), (wu, acc_u)):
            b = jnp.concatenate([w[j, e, cols] for e in range(2)], axis=0)
            v = jnp.dot(a, b, preferred_element_type=F32)
            if first:
                acc[at] = v
            else:
                acc[at] += v

    for q, (start, size) in enumerate(cuts):
        if q:
            all_slot_copies(q).wait_recv()
        all_slots = slots[q][:, :cap].reshape(MEMBERS * cap, size)
        for h in range(2):
            gath[q][spot_of(d, c, h)] = jnp.dot(
                pick[h * half:(h + 1) * half], all_slots, preferred_element_type=F32
            ).astype(BF16)
            if h == 0 or q == 0:
                send_piece(d, h, q, to_up)
            send_piece(d, h, q, to_down, to_across, to_core)

    aup, adown, far, afar = chip(True, 1), chip(True, 3), chip(False, 2), chip(True, 2)
    load_g.wait()
    load_u.wait()
    multiply(d, 0, 0, first=True)
    multiply(d, 0, 1, first=True)
    take_piece(down, 0, 0, to_up)
    take_piece(up, 1, 0, to_down)
    take_piece(up, 0, 0)
    take_piece(down, 1, 0)
    multiply(d, 1, 0)
    multiply(d, 1, 1)
    take_piece(across, 0, 0, to_up, to_down)
    take_piece(across, 1, 0, to_down)
    multiply(down, 0, 0)
    multiply(up, 0, 0)
    take_piece(across, 0, 1, to_up, to_down)
    take_piece(down, 0, 1, to_up)
    take_piece(up, 0, 1)
    multiply(across, 0, 0)
    multiply(across, 0, 1)
    multiply(down, 0, 1)
    multiply(up, 0, 1)
    take_piece(across, 1, 1, to_down)
    relay_on(0)
    for q in range(2):
        all_slot_copies(q).wait_send()
    take_piece(adown, 0, 0, to_up)
    take_piece(up, 1, 1, to_down)
    take_piece(far, 0, 0)
    multiply(across, 1, 0)
    multiply(down, 1, 0)
    multiply(up, 1, 0)
    multiply(far, 0, 0)

    take_piece(aup, 0, 0)
    take_piece(adown, 0, 1, to_up)
    send_piece(d, 1, 1, to_up)
    send_piece(across, 1, 0, to_up)
    send_piece(across, 1, 1, to_up)
    multiply(up, 1, 1)
    take_piece(aup, 1, 0, to_down)
    take_piece(far, 1, 0)
    multiply(across, 1, 1)
    multiply(adown, 0, 0)
    multiply(aup, 0, 0)
    multiply(adown, 1, 0)
    multiply(far, 0, 1)
    multiply(aup, 0, 1)
    relay_on(1)
    take_piece(far, 0, 1)
    take_piece(aup, 0, 1)
    take_piece(afar, 0, 0)
    multiply(far, 1, 0)
    multiply(aup, 1, 0)
    take_piece(aup, 1, 1, to_down)
    multiply(afar, 0, 0)
    take_piece(afar, 0, 1)
    multiply(aup, 1, 1)
    multiply(afar, 1, 0)

    def activate(h):
        def block(n):
            at = pl.ds(pl.multiple_of(h * half + n * 128, 128), 128)
            g = acc_g[at]
            hid[at] = (g / (1.0 + jnp.exp(-g)) * acc_u[at]).astype(BF16)

        loop(0, half // 128, block)

    FAR, UP, DOWN, HERE = range(4)
    steps = (2, 1, 3, 0)

    def core_copy(q, h, t):
        return remote(
            core_out.at[q, h, t], core_in.at[q, h, t], core_s.at[0], core_r.at[q, h, t], to_core
        )

    def project(q, h, *targets):
        cols = slice(q * LANES, (q + 1) * LANES)
        for t in targets:
            chips = (chip(True, steps[t]), chip(False, steps[t]))
            w = jnp.concatenate(
                [wd[j, e, :, cols] for j in chips for e in (1 - c, c)], axis=1
            )
            v = jnp.dot(hid[h * half:(h + 1) * half], w, preferred_element_type=F32)
            for g in range(2):
                core_out[q, h, t, g] = v[:, 2 * g * LANES:(2 * g + 1) * LANES].astype(BF16)
                own[q, h, t, g] = v[:, (2 * g + 1) * LANES:(2 * g + 2) * LANES]
            core_copy(q, h, t).start()

    def both(q, h, t):
        return own[q, h, t] + core_in[q, h, t].astype(F32)

    def far_copy(q, h):
        return remote(
            opp_out.at[q, h], opp_in.at[q, h], opp_s.at[0], opp_r.at[q, h],
            to_down if h else to_up,
        )

    def send_far(q, h):
        core_copy(q, h, FAR).wait_recv()
        opp_out[q, h] = both(q, h, FAR).astype(BF16)
        far_copy(q, h).start()

    last = (strips - 1, 1)

    def near_copies(q, h, way):
        device = to_down if way else to_up
        if (q, h) != last:
            return [remote(
                near_out.at[q, h, way], near_in.at[q, h, way],
                near_s.at[0], near_r.at[q, h, 0], device,
            )]
        return [
            remote(
                near_out.at[q, h, way, g], near_in.at[q, h, way, g],
                near_s.at[0], near_r.at[q, h, g], device,
            )
            for g in (1, 0)
        ]

    def send_near(q, h, way, v):
        near_out[q, h, way] = v.astype(BF16)
        for cp in near_copies(q, h, way):
            cp.start()

    def send_free(q, h):
        t = UP if h else DOWN
        core_copy(q, h, t).wait_recv()
        send_near(q, h, 1 - h, both(q, h, t))

    def send_joined(q, h):
        t = DOWN if h else UP
        core_copy(q, h, t).wait_recv()
        far_copy(q, h).wait_recv()
        send_near(q, h, h, both(q, h, t) + opp_in[q, h].astype(F32))

    def send_sum(q, h, g):
        remote(
            sum_out.at[q, h, g], sum_in.at[q, h, y], sum_s.at[0], sum_r.at[q, h],
            (after, c, d if g else across),
        ).start()

    def collect(q, h):
        core_copy(q, h, HERE).wait_recv()
        if (q, h) != last:
            remote(
                near_out.at[q, h], near_in.at[q, h], near_s.at[0], near_r.at[q, h, 0], to_up
            ).wait_recv()
            sum_out[q, h] = (
                both(q, h, HERE) + near_in[q, h, 0].astype(F32) + near_in[q, h, 1].astype(F32)
            ).astype(BF16)
            send_sum(q, h, 1)
            send_sum(q, h, 0)
            return
        for g in (1, 0):
            remote(
                near_out.at[q, h, :, g], near_in.at[q, h, :, g],
                near_s.at[0], near_r.at[q, h, g], to_up,
            ).wait_recv()
            sum_out[q, h, g] = (
                own[q, h, HERE, g] + core_in[q, h, HERE, g].astype(F32)
                + near_in[q, h, 0, g].astype(F32) + near_in[q, h, 1, g].astype(F32)
            ).astype(BF16)
            send_sum(q, h, g)

    def back_copy(k, q):
        i, device = member(k)
        return remote(
            back_out.at[q, i], back_in.at[q, me], back_s.at[q], back_r.at[q], device
        )

    def all_back_copies(q):
        block = pl.ds(0, MEMBERS - 1)
        return remote(
            back_out.at[q, block], back_in.at[q, block], back_s.at[q], back_r.at[q], to_core
        )

    sides = ((1 - y, CHIPS), (y, 0))

    def spread_rows(q, h, yy):
        final = (sum_in[q, h, 0].astype(F32) + sum_in[q, h, 1].astype(F32)).astype(BF16)
        at = pl.ds(pl.multiple_of(yy * (CHIPS * cap), CHIPS * cap), CHIPS * cap)
        return jnp.dot(
            place[at, h * half:(h + 1) * half], final, preferred_element_type=F32
        )

    def wait_sums(q, h):
        ref = sum_in.at[q, h]
        remote(ref, ref, sum_s.at[0], sum_r.at[q, h], to_core).wait_recv()

    def unpack_first(q):
        wait_sums(q, 0)
        for t, (yy, first) in enumerate(sides):
            partial[q % 2, t] = spread_rows(q, 0, yy)

    def unpack(q):
        wait_sums(q, 1)
        for t, (yy, first) in enumerate(sides):
            back_out[q, pl.ds(yy * CHIPS, CHIPS)] = (
                (partial[q % 2, t] + spread_rows(q, 1, yy))
                .astype(BF16)
                .reshape(CHIPS, cap, LANES)
            )
            for k in range(first + CHIPS - 1, max(first, 1) - 1, -1):
                back_copy(k, q).start()
        own_rows(q).start()

    def own_rows(q):
        return pltpu.make_async_copy(back_out.at[q, me], back_in.at[q, me], out_sem.at[q])

    activate(0)
    pltpu.make_async_copy(wd, wd, load_sem.at[2]).wait()
    project(0, 0, FAR, DOWN, UP)
    take_piece(far, 1, 1)
    take_piece(down, 1, 1)
    send_far(0, 0)
    send_free(0, 0)
    project(0, 0, HERE)
    relay_on(2)
    project(1, 0, FAR, DOWN, UP)
    take_piece(afar, 1, 0)
    take_piece(adown, 1, 0)
    multiply(far, 1, 1)
    send_far(1, 0)
    send_free(1, 0)
    multiply(down, 1, 1)
    multiply(afar, 0, 1)
    multiply(adown, 0, 1)
    project(1, 0, HERE)
    project(2, 0, FAR, DOWN, UP)
    take_piece(afar, 1, 1)
    take_piece(adown, 1, 1)
    send_far(2, 0)
    send_free(2, 0)
    project(2, 0, HERE)
    relay_on(3)
    multiply(afar, 1, 1)
    multiply(adown, 1, 1)
    activate(1)
    send_joined(0, 0)
    project(0, 1, FAR, UP, DOWN)
    send_far(0, 1)
    project(0, 1, HERE)
    project(1, 1, FAR)
    send_joined(1, 0)
    send_free(0, 1)
    project(1, 1, UP, DOWN)
    send_far(1, 1)
    project(1, 1, HERE)
    project(2, 1, FAR)
    send_joined(2, 0)
    send_free(1, 1)
    project(2, 1, UP, DOWN)
    send_free(2, 1)
    project(2, 1, HERE)

    relay_counts.wait_recv()
    off = jnp.zeros((1, LANES), F32)
    s_i, r_i = iota((cap, rows), 0), iota((cap, rows), 1)
    for i in range(MEMBERS):
        n = counts_in[i].astype(F32)[0:1]
        hit = (r_i - s_i == off[:, 0:1]) & (s_i < n[:, 0:1])
        place[i * cap:(i + 1) * cap] = jnp.where(hit, 1.0, 0.0).astype(BF16)
        off = off + n

    collect(0, 0)
    send_joined(0, 1)
    send_far(2, 1)
    collect(1, 0)
    send_joined(1, 1)
    collect(0, 1)
    send_joined(2, 1)
    collect(2, 0)
    collect(1, 1)
    collect(2, 1)
    unpack_first(0)
    unpack(0)
    unpack_first(1)
    unpack_first(2)
    unpack(1)
    unpack(2)
    relay_route.wait_recv()
    relay_x = remote(x_mid, x_in, relay_s.at[3], relay_r.at[2], to_across)
    relay_x.wait_recv()
    for q in range(2):
        gather_sent(q)
    for src, dst, sem in (
        (core_out, core_in, core_s), (opp_out, opp_in, opp_s),
        (near_out, near_in, near_s), (sum_out, sum_in, sum_s),
    ):
        remote(src, dst, sem.at[0], relay_r.at[0], to_core).wait_send()
    relay_first = remote(x_v, x_mid, relay_s.at[2], mid_r.at[0], to_across)
    for cp in (relay_route, relay_counts, relay_first, relay_x):
        cp.wait_send()
    for q in range(strips):
        own_rows(q).wait()
        all_back_copies(q).wait_recv()
        all_back_copies(q).wait_send()


def finish(x_hbm, back_hbm, route_hbm, out_hbm, x_v, back_v, route_v, out_v, in_sem, out_sem):
    strips, owners, cap, lanes = back_v.shape
    part = strips * lanes
    width = x_v.shape[1] // FINISH_STEPS
    count = owners // FINISH_STEPS
    load_route = pltpu.make_async_copy(route_hbm, route_v, in_sem.at[0])
    load_route.start()
    loads, stores = [], []
    for i in range(FINISH_STEPS):
        at, ks = pl.ds(i * width, width), pl.ds(i * count, count)
        pair = (
            pltpu.make_async_copy(back_hbm.at[:, ks], back_v.at[:, ks], in_sem.at[1 + 2 * i]),
            pltpu.make_async_copy(x_hbm.at[:, at], x_v.at[:, at], in_sem.at[2 + 2 * i]),
        )
        for cp in pair:
            cp.start()
        loads.append(pair)
        stores.append(pltpu.make_async_copy(out_v.at[:, at], out_hbm.at[:, at], out_sem.at[i]))
    load_route.wait()
    spread = route_v[:, :cap].astype(BF16)
    weight = route_v[:, cap:cap + 1]
    for i in range(FINISH_STEPS):
        for cp in loads[i]:
            cp.wait()
        for k in range(i * count, (i + 1) * count):
            rows = jnp.concatenate([back_v[q, k] for q in range(strips)], axis=1)
            term = weight * jnp.dot(spread, rows, preferred_element_type=F32)
            at = slice(k * part, (k + 1) * part)
            out_v[:, at] = (x_v[:, at].astype(F32) + term).astype(BF16)
        stores[i].start()
    for cp in stores:
        cp.wait()


def solution(mesh):
    sections = mesh.shape["pipe"]

    def per_device(hidden_in, norm_gain, w_gate, w_up, w_down, expert_ids, gate_weights):
        tokens, width = hidden_in.shape
        ff = w_gate.shape[2]
        cap = tokens // 2
        rows = MEMBERS * cap // 2
        half = rows // 2
        part = width // MEMBERS
        strips = part // LANES
        vmem = pltpu.VMEM
        dma = pltpu.SemaphoreType.DMA
        any_space = pl.BlockSpec(memory_space=pl.ANY)
        x_in, back, route = pl.pallas_call(
            functools.partial(kernel, sections),
            out_shape=(
                jax.ShapeDtypeStruct((tokens, width), BF16),
                jax.ShapeDtypeStruct((strips, MEMBERS, cap, LANES), BF16),
                jax.ShapeDtypeStruct((tokens, tokens), F32),
            ),
            in_specs=[any_space] * 7,
            out_specs=(any_space,) * 3,
            scratch_shapes=[
                vmem((tokens, width), BF16),
                vmem((tokens, width), BF16),
                vmem((1, width), F32),
                vmem((2, tokens), jnp.int32),
                vmem((2, tokens), F32),
                vmem((tokens, tokens), F32),
                vmem((MEMBERS, TILE, LANES), BF16),
                vmem((MEMBERS, TILE, LANES), BF16),
                vmem((CHIPS, 2, part, ff), BF16),
                vmem((CHIPS, 2, part, ff), BF16),
                vmem((CHIPS, 2, ff, part), BF16),
                vmem((MEMBERS, cap + TILE, LANES), BF16),
                vmem((MEMBERS, cap, part - LANES), BF16),
                vmem((MEMBERS, cap + TILE, LANES), BF16),
                vmem((MEMBERS, cap, part - LANES), BF16),
                vmem((rows, MEMBERS * cap), BF16),
                vmem((MEMBERS * cap, rows), BF16),
                vmem((CHIPS * 4, half, LANES), BF16),
                vmem((CHIPS * 4, half, part - LANES), BF16),
                vmem((rows, ff), F32),
                vmem((rows, ff), F32),
                vmem((rows, ff), BF16),
                vmem((strips, 2, 4, 2, half, LANES), F32),
                vmem((strips, 2, 4, 2, half, LANES), BF16),
                vmem((strips, 2, 4, 2, half, LANES), BF16),
                vmem((strips, 2, 2, half, LANES), BF16),
                vmem((strips, 2, 2, half, LANES), BF16),
                vmem((strips, 2, 2, 2, half, LANES), BF16),
                vmem((strips, 2, 2, 2, half, LANES), BF16),
                vmem((strips, 2, 2, half, LANES), BF16),
                vmem((strips, 2, 2, half, LANES), BF16),
                vmem((2, 2, CHIPS * cap, LANES), F32),
                vmem((strips, MEMBERS, cap, LANES), BF16),
                dma((6 + X_LOADS,)), dma((strips,)),
                dma((2,)), dma((2,)),
                dma((2,)), dma((2, CHIPS, 2)), dma((2, CHIPS, 2)),
                dma((1,)), dma((strips, 2, 4)),
                dma((1,)), dma((strips, 2)),
                dma((1,)), dma((strips, 2, 2)),
                dma((1,)), dma((strips, 2)),
                dma((strips,)), dma((strips,)),
                dma((4,)), dma((3,)), dma((RELAY_PIECES,)),
            ],
            compiler_params=pltpu.CompilerParams(
                collective_id=0, has_side_effects=True, vmem_limit_bytes=62 * 2**20
            ),
            name="routed_block",
        )(
            hidden_in,
            norm_gain,
            w_gate.reshape(CHIPS, 2, part, ff),
            w_up.reshape(CHIPS, 2, part, ff),
            w_down.reshape(ff, width),
            expert_ids.T,
            gate_weights.T,
        )
        in_hbm = pl.BlockSpec(memory_space=pltpu.HBM)
        return pl.pallas_call(
            finish,
            out_shape=jax.ShapeDtypeStruct((tokens, width), BF16),
            in_specs=[in_hbm] * 3,
            out_specs=in_hbm,
            scratch_shapes=[
                vmem((tokens, width), BF16),
                vmem((strips, MEMBERS, cap, LANES), BF16),
                vmem((tokens, tokens), F32),
                vmem((tokens, width), BF16),
                dma((1 + 2 * FINISH_STEPS,)),
                dma((FINISH_STEPS,)),
            ],
            compiler_params=pltpu.CompilerParams(vmem_limit_bytes=62 * 2**20),
            name="add_rows",
        )(x_in, back, route)

    return jax.shard_map(
        per_device,
        mesh=mesh,
        in_specs=(
            P(("pipe", "expert", "dp"), None),
            P("pipe", None),
            P("pipe", None, ("expert", "dp")),
            P("pipe", None, ("expert", "dp")),
            P("pipe", ("expert", "dp"), None),
            P(("pipe", "expert", "dp"), None),
            P(("pipe", "expert", "dp"), None),
        ),
        out_specs=P(("pipe", "expert", "dp"), None),
        check_vma=False,
    )
```
